128 devices in a mesh: mem: 32 (over x, z, core), feat: 4 (over y).
Axes of the slice: x: 4, y: 4, z: 4, core: 2. Of those that a mesh axis runs over, the one named last changes fastest.
Arguments:
- events: bfloat16 [8192, 32, 256], P('mem'), may hold values from -6 to 6
- w_in: bfloat16 [256, 1024], P(None, 'feat'), may hold values from -0.375 to 0.375
- w_out: bfloat16 [1024, 256], P('feat'), may hold values from -0.1875 to 0.1875
- probe_vectors: bfloat16 [8192, 256], P(('mem', 'feat')), may hold values from -8 to 8
- key_queue: bfloat16 [262144, 256], P('mem'), may hold values from -1 to 1
- target_position: int32 [8192], P(('mem', 'feat')), may hold values from 0 to 262143
- pointer: int32 [1], replicated, may hold values from 0 to 262143
Outputs:
- loss: float32 [8192], P(('mem', 'feat'))
- probe_derivative: float32 [8192, 256], P(('mem', 'feat'))
- new_memory: bfloat16 [262144, 256], P('mem')
The draws below stay inside these ranges and needn't reach their ends.
All inputs are finite; a program needn't handle non-finite values.
Results may differ from the reference program's by a relative error of at most 0.0017.
Values may be sent and summed in bfloat16 or wider, within the bound.
No kernel may reach another device: no remote copies, remote signals or barrier semaphores. Data moves between devices by JAX's collectives and lax.ppermute only.
A program may use at most 64 MiB of HBM per device.

```python
import jax
import jax.numpy as jnp
from jax import lax

D = 256
HID = 1024
EVENTS = 32
SESS_DEV = 256
SLOT_DEV = 8192
QUERIES = 8192
SESSIONS = 8192
SLOTS = 262144
N_MEM = 32


def shared_directions(key):
    norm_factor = 1.0 / jnp.sqrt(jnp.float32(D))
    first = jax.random.truncated_normal(jax.random.fold_in(key, 7), -6.0, 6.0, (16, D), jnp.float32) * norm_factor
    second = jax.random.truncated_normal(jax.random.fold_in(key, 8), -6.0, 6.0, (16, D), jnp.float32) * norm_factor
    first = jnp.clip(first, -0.9, 0.9)
    second = jnp.clip(second, -0.9, 0.9)
    return (first, 0.99 * first + 0.1 * second)


def draw_key_queue(key, part):
    values_drawn = jax.random.truncated_normal(jax.random.fold_in(key, 1), -6.0, 6.0, (SLOTS, D), jnp.float32) / 16.0
    first, twins = shared_directions(key)
    planted_rows = jnp.arange(16, dtype=jnp.int32) * (SLOTS // 16) + 3
    values_drawn = values_drawn.at[planted_rows].set(first)
    values_drawn = values_drawn.at[planted_rows + SLOTS // 32 + 5].set(twins)
    return jnp.clip(values_drawn, -1.0, 1.0).astype(jnp.bfloat16)


def draw_probe_vectors(key, part):
    values_drawn = jax.random.truncated_normal(jax.random.fold_in(key, 2), -6.0, 6.0, (QUERIES, D), jnp.float32) * 0.25
    first, twins = shared_directions(key)
    planted_rows = jnp.arange(16, dtype=jnp.int32) * (QUERIES // 16)
    strength = 9.0 + 9.0 * jnp.arange(16, dtype=jnp.float32) / 15.0
    values_drawn = values_drawn.at[planted_rows].set(jnp.clip(strength[:, None] * first, -8.0, 8.0))
    return values_drawn.astype(jnp.bfloat16)


def touch_ends(drawn, stream_key, low, high):
    extent = drawn.shape
    index_at = [jax.random.randint(jax.random.fold_in(stream_key, axis), (), 0, extent[axis]) for axis in range(len(extent))]
    drawn = drawn.at[tuple(index_at)].set(low)
    longest = extent.index(max(extent))
    index_at[longest] = (index_at[longest] + 1) % extent[longest]
    return drawn.at[tuple(index_at)].set(high)


def levels(own_key, dims, split, low, top_value):
    gain, own = 1.0, jax.random.fold_in(own_key, 6)
    for axis_at, shards_of in split:
        steps = jnp.exp(jax.random.uniform(jax.random.fold_in(own, axis_at), (shards_of,), jnp.float32, low / len(split), top_value / len(split)))
        gain = gain * jnp.repeat(steps, dims[axis_at] // shards_of).reshape([-1 if axis == axis_at else 1 for axis in range(len(dims))])
    return gain


def gaussian(rng, dims, spread, limit, cuts=(), kind=jnp.bfloat16):
    drawn = jax.random.normal(rng, dims, jnp.float32) * spread
    if len(cuts) > 0:
        drawn = levels(rng, dims, cuts, -0.22, 0.18) * drawn
    return jnp.clip(drawn, min=-limit, max=limit).astype(kind)


def setup_inputs(seed: int = 0) -> dict:
    arg_keys = jax.random.split(jax.random.key(seed), 8)
    return {
        "events": gaussian(arg_keys[0], (SESSIONS, EVENTS, D), 1.0, 6.0, ((0, 32),)),
        "w_in": gaussian(arg_keys[1], (D, HID), D ** -0.5, 0.375, ((1, 4),)),
        "w_out": gaussian(arg_keys[2], (HID, D), HID ** -0.5, 0.1875, ((0, 4),)),
        "probe_vectors": draw_probe_vectors(jax.random.fold_in(arg_keys[7], 71), 0),
        "key_queue": draw_key_queue(jax.random.fold_in(arg_keys[7], 71), 0),
        "target_position": touch_ends(jax.random.randint(arg_keys[5], (QUERIES,), 0, SLOTS), jax.random.fold_in(arg_keys[5], 1), 0, SLOTS - 1).astype(jnp.int32),
        "pointer": jax.random.randint(arg_keys[6], (1,), 0, SLOTS).astype(jnp.int32),
    }


inverse_softness = 14.0
epsilon = 1e-06

def encode_block(session_block, w_in, w_out):
    flattened = session_block.reshape(session_block.shape[0] * EVENTS, D)
    activation = jax.nn.gelu(jnp.dot(flattened, w_in, preferred_element_type=jnp.float32))
    pooled = lax.optimization_barrier(jnp.mean(activation.reshape(session_block.shape[0], EVENTS, HID), axis=1)).astype(jnp.bfloat16)
    raw_key = jnp.dot(pooled, w_out, preferred_element_type=jnp.float32)
    scaled = raw_key * lax.rsqrt(lax.optimization_barrier(jnp.mean(raw_key * raw_key, axis=1, keepdims=True)) + epsilon) / 16.0
    return scaled.astype(jnp.bfloat16)

def reference(events, w_in, w_out, probe_vectors, key_queue, target_position, pointer):

    def encode_one(session_block):
        return encode_block(session_block, w_in, w_out)
    keys = lax.map(encode_one, events.reshape(N_MEM, SESS_DEV, EVENTS, D)).reshape(N_MEM * SESS_DEV, D)
    query_count = probe_vectors.shape[0]
    slot_blocks = key_queue.reshape(N_MEM, SLOT_DEV, D)
    block_starts = jnp.arange(N_MEM, dtype=jnp.int32) * SLOT_DEV
    positions = jnp.arange(SLOT_DEV, dtype=jnp.int32)

    def first_pass(carry, item):
        running_max, running_sum, positive_score = carry
        queue_position_span, first_slot = item
        similarity_table = jnp.dot(probe_vectors, queue_position_span.T, preferred_element_type=jnp.float32) * inverse_softness
        new_max = jnp.maximum(running_max, lax.optimization_barrier(jnp.max(similarity_table, axis=1)))
        running_sum = running_sum * jnp.exp(running_max - new_max) + lax.optimization_barrier(jnp.sum(jnp.exp(similarity_table - new_max[:, None]), axis=1))
        hit = positions[None, :] == (target_position - first_slot)[:, None]
        positive_score = positive_score + lax.optimization_barrier(jnp.sum(jnp.where(hit, similarity_table, 0.0), axis=1))
        return ((new_max, running_sum, positive_score), None)
    start_carry = (jnp.full((query_count,), -jnp.inf, jnp.float32), jnp.zeros((query_count,), jnp.float32), jnp.zeros((query_count,), jnp.float32))
    (top, total, positive_score), unused = lax.scan(first_pass, start_carry, (slot_blocks, block_starts))
    loss = top + jnp.log(total) - positive_score

    def second_pass(collected_denominator, queue_position_span):
        similarity_table = jnp.dot(probe_vectors, queue_position_span.T, preferred_element_type=jnp.float32) * inverse_softness
        weights = (jnp.exp(similarity_table - top[:, None]) / total[:, None]).astype(jnp.bfloat16)
        return (collected_denominator + jnp.dot(weights, queue_position_span, preferred_element_type=jnp.float32), None)
    collected_denominator, unused = lax.scan(second_pass, jnp.zeros((query_count, D), jnp.float32), slot_blocks)
    probe_derivative = inverse_softness * (collected_denominator - jnp.take(key_queue, target_position, axis=0).astype(jnp.float32))
    slot_count = N_MEM * SLOT_DEV
    slot_ids = jnp.arange(slot_count, dtype=jnp.int32)
    offsets = (slot_ids - pointer[0]) % slot_count
    picked = jnp.take(keys, jnp.minimum(offsets, keys.shape[0] - 1), axis=0)
    new_memory = jnp.where((offsets < keys.shape[0])[:, None], picked, key_queue)
    return (loss, probe_derivative, new_memory)
```

```python
import functools

import jax
import jax.numpy as jnp
from jax import lax
from jax.experimental import pallas as pl
from jax.experimental.pallas import tpu as pltpu
from jax.sharding import Mesh
from jax.sharding import PartitionSpec as P

f32 = jnp.float32
bf16 = jnp.bfloat16
SOFT = 14.0
LOG2E = 1.4426950408889634
LN2 = 0.6931471805599453
C2 = SOFT * LOG2E
EPS = 1e-06
D = 256
EV = 32
OWN = 64
GRP = 256
SLOTS = 8192
SESS = 256
SIZES = (4, 4, 2, 4)
ALL = ("x", "z", "c", "f")
ML = 64
POS = 72
PIECE = 136
BIG = 2.0**90
CONTRACT_LAST = (((1,), (1,)), ((), ()))
VMEM_LIMIT = 50 << 20


def flat(p):
    return ((p[0] * SIZES[1] + p[1]) * SIZES[2] + p[2]) * SIZES[3] + p[3]


def ring(axes, step):
    pairs = []
    for x in range(SIZES[0]):
        for z in range(SIZES[1]):
            for c in range(SIZES[2]):
                for f in range(SIZES[3]):
                    p = [x, z, c, f]
                    k = "xzcf".index(axes[c])
                    p[k] = (p[k] + step) % SIZES[k]
                    pairs.append((flat((x, z, c, f)), flat(p)))
    return pairs


def shift(a, axes, step):
    return lax.ppermute(a, ALL, ring(axes, step % 4))


def swap_cores(a):
    return lax.ppermute(a, "c", [(0, 1), (1, 0)])


def encoder_kernel(ev_ref, w_in_ref, w_out_ref, out_ref, pooled_ref):
    i = pl.program_id(0)
    sessions = ev_ref.shape[0]
    rows = 8
    for s in range(0, sessions, rows):
        x = jnp.dot(
            ev_ref[s : s + rows].reshape(rows * EV, D), w_in_ref[...], preferred_element_type=f32
        )
        inner = x * (0.7978845608028654 + 0.035677408136300125 * (x * x))
        g = x + x * jnp.tanh(inner)
        pooled_ref[pl.ds(i * sessions + s, rows), :] = jnp.sum(
            g.reshape(rows, EV, D), axis=1
        ) * (0.5 / EV)

    @pl.when(i == pl.num_programs(0) - 1)
    def _():
        out_ref[...] = jnp.dot(
            pooled_ref[...].astype(bf16), w_out_ref[...], preferred_element_type=f32
        )


def encode(events, w_in, w_out):
    step = 32
    return pl.pallas_call(
        encoder_kernel,
        grid=(SESS // step,),
        in_specs=[
            pl.BlockSpec((step, EV, D), lambda i: (i, 0, 0)),
            pl.BlockSpec((D, D), lambda i: (0, 0)),
            pl.BlockSpec((D, D), lambda i: (0, 0)),
        ],
        out_specs=pl.BlockSpec((SESS, D), lambda i: (0, 0)),
        out_shape=jax.ShapeDtypeStruct((SESS, D), f32),
        scratch_shapes=[pltpu.VMEM((SESS, D), f32)],
        compiler_params=pltpu.CompilerParams(vmem_limit_bytes=VMEM_LIMIT),
        cost_estimate=pl.CostEstimate(
            flops=2 * SESS * EV * D * D, bytes_accessed=4 << 20, transcendentals=SESS * EV * D
        ),
        name="encoder",
    )(events, w_in, w_out)


def keys_kernel(ptr_ref, a_ref, b_ref, c_ref, d_ref, out_ref):
    raw = (a_ref[...] + b_ref[...]) + (c_ref[...] + d_ref[...])
    scale = lax.rsqrt(jnp.mean(raw * raw, axis=1, keepdims=True) + EPS)
    keys = (raw * scale / 16.0).astype(bf16)
    turn = lax.rem(ptr_ref[0], SESS)
    row = lax.broadcasted_iota(jnp.int32, (SESS, SESS), 0)
    col = lax.broadcasted_iota(jnp.int32, (SESS, SESS), 1)
    source = row - turn
    source = jnp.where(source < 0, source + SESS, source)
    pick = jnp.where(col == source, 1.0, 0.0).astype(bf16)
    out_ref[...] = jnp.dot(pick, keys, preferred_element_type=f32).astype(bf16)


def finish_keys(pointer, parts):
    return pl.pallas_call(
        keys_kernel,
        in_specs=[pl.BlockSpec(memory_space=pltpu.SMEM)]
        + [pl.BlockSpec(memory_space=pltpu.VMEM)] * 4,
        out_specs=pl.BlockSpec(memory_space=pltpu.VMEM),
        out_shape=jax.ShapeDtypeStruct((SESS, D), bf16),
        cost_estimate=pl.CostEstimate(flops=1 << 26, bytes_accessed=2 << 20, transcendentals=0),
        name="finish_keys",
    )(pointer, *parts)


def diagonal(n):
    return lax.broadcasted_iota(jnp.int32, (n, n), 0) == lax.broadcasted_iota(
        jnp.int32, (n, n), 1
    )


def to_row(col, eye):
    return jnp.sum(jnp.where(eye, jnp.broadcast_to(col, eye.shape), 0.0), axis=0, keepdims=True)


def to_col(row, eye):
    return jnp.sum(jnp.where(eye, jnp.broadcast_to(row, eye.shape), 0.0), axis=1, keepdims=True)


CHUNKS = ((0, 0, 512), (0, 512, 1536), (0, 2048, 2048), (0, 4096, 4096), (1, 0, 4096), (1, 4096, 4096))
SB = 512


def attend_kernel(loc_ref, q_ref, k0_ref, k1_ref, out_ref, kbuf, q2, m_ref, l_ref, acc, todo, sems):
    copies = []
    for n, (which, first, rows) in enumerate(CHUNKS):
        src = (k0_ref, k1_ref)[which]
        copy = pltpu.make_async_copy(
            src.at[pl.ds(first, rows)],
            kbuf.at[pl.ds(which * SLOTS + first, rows)],
            sems.at[n],
        )
        copy.start()
        copies.append((which * SLOTS + first, copy))
    for j in range(4):
        q2[j * OWN : (j + 1) * OWN, :] = q_ref[j, :OWN, :]

    def score(b):
        return lax.dot_general(
            q2[...], kbuf[b : b + SB, :], CONTRACT_LAST, preferred_element_type=f32
        )

    copies[0][1].wait()
    s = score(0)
    m_ref[...] = jnp.broadcast_to(jnp.max(s, axis=1, keepdims=True) * C2, (GRP, 128))
    l_ref[...] = jnp.zeros_like(l_ref)
    acc[...] = jnp.zeros_like(acc)
    waiting = copies[1:]
    total = 2 * SLOTS
    for b in range(0, total, SB):
        if b + SB < total:
            if waiting and waiting[0][0] == b + SB:
                waiting.pop(0)[1].wait()
            following = score(b + SB)
        m = m_ref[...]
        l = l_ref[...]
        ps = []
        for j in range(0, SB, 128):
            p = jnp.exp2(s[:, j : j + 128] * C2 - m)
            l = l + p
            ps.append(p.astype(bf16))
        l_ref[...] = l
        acc[...] += jnp.dot(
            jnp.concatenate(ps, axis=1), kbuf[b : b + SB, :], preferred_element_type=f32
        )
        s = following

    @pl.when(jnp.logical_not(jnp.max(l_ref[...]) < BIG))
    def _():
        m_ref[...] = jnp.full_like(m_ref, -3.0e38)
        l_ref[...] = jnp.zeros_like(l_ref)
        acc[...] = jnp.zeros_like(acc)

        def again(n, carry):
            block = kbuf[pl.ds(pl.multiple_of(n * SB, SB), SB), :]
            t = lax.dot_general(q2[...], block, CONTRACT_LAST, preferred_element_type=f32) * C2
            old = m_ref[...]
            new = jnp.maximum(old, jnp.max(t, axis=1, keepdims=True))
            keep = jnp.exp2(old - new)
            p = jnp.exp2(t - new[:, :1])
            part = p[:, :128]
            for j in range(128, SB, 128):
                part = part + p[:, j : j + 128]
            l_ref[...] = l_ref[...] * keep + part
            acc[...] = acc[...] * keep[:, :1] + jnp.dot(
                p.astype(bf16), block, preferred_element_type=f32
            )
            m_ref[...] = new
            return carry

        lax.fori_loop(0, total // SB, again, 0)

    eye = diagonal(OWN)
    lane_pad = jnp.zeros((1, D - OWN), f32)
    for j in range(4):
        rows = slice(j * OWN, (j + 1) * OWN)
        out_ref[j, :OWN, :] = acc[rows, :]
        m_row = to_row(m_ref[rows, :1], eye)
        l_row = to_row(jnp.sum(l_ref[rows, :], axis=1, keepdims=True), eye)
        out_ref[j, ML:POS, :] = jnp.concatenate(
            [
                jnp.concatenate([m_row, lane_pad], axis=1),
                jnp.concatenate([l_row, lane_pad], axis=1),
                jnp.zeros((6, D), f32),
            ],
            axis=0,
        )
        out_ref[j, POS:PIECE, :] = jnp.zeros((OWN, D), f32)

    def note(i, n):
        t = loc_ref[i]
        todo[n] = t * GRP + i
        return n + jnp.where(t >= 0, 1, 0)

    count = lax.fori_loop(0, GRP, note, 0, unroll=8)

    def fetch(j, carry):
        entry = todo[j]
        i = entry & (GRP - 1)
        t = entry >> 8
        group = kbuf[pl.ds(pl.multiple_of((t >> 4) << 4, 16), 16), :].astype(f32)
        hit = lax.broadcasted_iota(jnp.int32, (16, D), 0) == (t & 15)
        out_ref[i >> 6, pl.ds(POS + (i & 63), 1), :] = jnp.sum(
            jnp.where(hit, group, 0.0), axis=0, keepdims=True
        )
        return carry

    lax.fori_loop(0, count, fetch, 0)


def attend(loc, q, k_own, k_other):
    return pl.pallas_call(
        attend_kernel,
        in_specs=[
            pl.BlockSpec(memory_space=pltpu.SMEM),
            pl.BlockSpec(memory_space=pltpu.VMEM),
            pl.BlockSpec(memory_space=pl.ANY),
            pl.BlockSpec(memory_space=pl.ANY),
        ],
        out_specs=pl.BlockSpec(memory_space=pltpu.VMEM),
        out_shape=jax.ShapeDtypeStruct((4, PIECE, D), f32),
        scratch_shapes=[
            pltpu.VMEM((2 * SLOTS, D), bf16),
            pltpu.VMEM((GRP, D), bf16),
            pltpu.VMEM((GRP, 128), f32),
            pltpu.VMEM((GRP, 128), f32),
            pltpu.VMEM((GRP, D), f32),
            pltpu.SMEM((GRP + 8,), jnp.int32),
            pltpu.SemaphoreType.DMA((len(CHUNKS),)),
        ],
        compiler_params=pltpu.CompilerParams(vmem_limit_bytes=VMEM_LIMIT),
        cost_estimate=pl.CostEstimate(
            flops=8 * GRP * SLOTS * D, bytes_accessed=9 << 20, transcendentals=2 * GRP * SLOTS
        ),
        name="attend",
    )(loc, q, k_own, k_other)


def combine(pieces, eye):
    ms = [p[ML : ML + 1, :OWN] for p in pieces]
    top = functools.reduce(jnp.maximum, ms)
    scales = [jnp.exp2(m - top) for m in ms]
    total = sum(p[ML + 1 : ML + 2, :OWN] * s for p, s in zip(pieces, scales))
    return top, scales, total


def merge_kernel(a_ref, b_ref, c_ref, d_ref, *outs):
    eye = diagonal(OWN)
    lane_pad = jnp.zeros((1, D - OWN), f32)
    for j in range(4):
        refs = [r.at[j] for r in (a_ref, b_ref, c_ref, d_ref)]
        top, scales, total = combine(refs, eye)
        o = outs[j]
        o[:OWN, :] = sum(r[:OWN, :] * to_col(s, eye) for r, s in zip(refs, scales))
        o[ML:POS, :] = jnp.concatenate(
            [
                jnp.concatenate([top, lane_pad], axis=1),
                jnp.concatenate([total, lane_pad], axis=1),
                jnp.zeros((6, D), f32),
            ],
            axis=0,
        )
        o[POS:PIECE, :] = sum(r[POS:PIECE, :] for r in refs)


def merge(states):
    return pl.pallas_call(
        merge_kernel,
        in_specs=[pl.BlockSpec(memory_space=pltpu.VMEM)] * 4,
        out_specs=[pl.BlockSpec(memory_space=pltpu.VMEM)] * 4,
        out_shape=[jax.ShapeDtypeStruct((PIECE, D), f32)] * 4,
        compiler_params=pltpu.CompilerParams(vmem_limit_bytes=VMEM_LIMIT),
        cost_estimate=pl.CostEstimate(flops=1 << 22, bytes_accessed=3 << 20, transcendentals=4096),
        name="merge",
    )(*states)


def final_kernel(q_ref, a_ref, b_ref, c_ref, d_ref, loss_ref, grad_ref):
    eye = diagonal(OWN)
    refs = (a_ref, b_ref, c_ref, d_ref)
    top, scales, total = combine(refs, eye)
    inverse = 1.0 / total
    acc = sum(r[:OWN, :] * to_col(s * inverse, eye) for r, s in zip(refs, scales))
    positive = sum(r[POS:PIECE, :] for r in refs)
    grad_ref[...] = SOFT * (acc - positive)
    score = SOFT * jnp.sum(q_ref[...].astype(f32) * positive, axis=1, keepdims=True)
    loss_ref[...] = top * LN2 + jnp.log(total) - to_row(score, eye)


def finish(q, pieces):
    loss, grad = pl.pallas_call(
        final_kernel,
        in_specs=[pl.BlockSpec(memory_space=pltpu.VMEM)] * 5,
        out_specs=[pl.BlockSpec(memory_space=pltpu.VMEM)] * 2,
        out_shape=[jax.ShapeDtypeStruct((1, OWN), f32), jax.ShapeDtypeStruct((OWN, D), f32)],
        cost_estimate=pl.CostEstimate(flops=1 << 20, bytes_accessed=1 << 20, transcendentals=1024),
        name="finish",
    )(q, *pieces)
    return loss.reshape(OWN), grad


BLK = SESS
NBLK = SLOTS // BLK


def memory_kernel(info_ref, keys_ref, k_ref, out_ref, rbuf, kbuf, obuf, gsem, ksem, osem):
    pointer, me = info_ref[0], info_ref[1]
    r = lax.rem(pointer, SLOTS)
    first = lax.div(pointer, SLOTS)
    second = lax.rem(first + 1, 32)
    turn = lax.div(r, BLK)
    inner = lax.rem(r, BLK)
    is_first, is_second = me == first, me == second

    def needs_new(b):
        return jnp.logical_or(
            jnp.logical_and(is_first, (b + 1) * BLK > r), jnp.logical_and(is_second, b * BLK < r)
        )

    def needs_old(b):
        return jnp.logical_not(
            jnp.logical_or(
                jnp.logical_and(is_first, b * BLK >= r),
                jnp.logical_and(is_second, (b + 1) * BLK <= r),
            )
        )

    def new_copy(slot):
        block = lax.rem(slot - 1 - turn + 2 * NBLK, NBLK)
        return pltpu.make_async_copy(
            keys_ref.at[pl.ds(pl.multiple_of(block * BLK, BLK), BLK)],
            rbuf.at[pl.ds(slot * BLK, BLK)],
            gsem.at[slot],
        )

    def new_wanted(slot):
        wanted = []
        if slot > 0:
            wanted.append(needs_new(slot - 1))
        if slot < NBLK:
            wanted.append(needs_new(slot))
        return functools.reduce(jnp.logical_or, wanted)

    def old_copy(b):
        rows = pl.ds(b * BLK, BLK)
        return pltpu.make_async_copy(k_ref.at[rows], kbuf.at[rows], ksem.at[b])

    def out_copy(b):
        rows = pl.ds(b * BLK, BLK)
        return pltpu.make_async_copy(obuf.at[rows], out_ref.at[rows], osem.at[b])

    for slot in range(NBLK + 1):

        @pl.when(new_wanted(slot))
        def _():
            new_copy(slot).start()

        if slot < NBLK:

            @pl.when(needs_old(slot))
            def _():
                old_copy(slot).start()

    @pl.when(new_wanted(0))
    def _():
        new_copy(0).wait()

    row = lax.broadcasted_iota(jnp.int32, (BLK, D), 0)
    for b in range(NBLK):

        @pl.when(new_wanted(b + 1))
        def _():
            new_copy(b + 1).wait()

        @pl.when(needs_old(b))
        def _():
            old_copy(b).wait()

        rows = slice(b * BLK, (b + 1) * BLK)

        @pl.when(needs_new(b))
        def _():
            earlier = row < inner
            at = row + b * BLK
            take = jnp.logical_or(
                jnp.logical_and(is_first, at >= r), jnp.logical_and(is_second, at < r)
            )
            fresh = jnp.where(
                earlier,
                rbuf[rows, :].astype(f32),
                rbuf[(b + 1) * BLK : (b + 2) * BLK, :].astype(f32),
            )
            obuf[rows, :] = jnp.where(take, fresh, kbuf[rows, :].astype(f32)).astype(bf16)

        @pl.when(jnp.logical_not(needs_new(b)))
        def _():
            obuf[rows, :] = kbuf[rows, :]

        out_copy(b).start()
    for b in range(NBLK):
        out_copy(b).wait()


def new_memory_of(info, keys, key_queue):
    anywhere = pl.BlockSpec(memory_space=pl.ANY)
    return pl.pallas_call(
        memory_kernel,
        in_specs=[pl.BlockSpec(memory_space=pltpu.SMEM), anywhere, anywhere],
        out_specs=anywhere,
        out_shape=jax.ShapeDtypeStruct((SLOTS, D), bf16),
        scratch_shapes=[
            pltpu.VMEM((SLOTS + BLK, D), bf16),
            pltpu.VMEM((SLOTS, D), bf16),
            pltpu.VMEM((SLOTS, D), bf16),
            pltpu.SemaphoreType.DMA((NBLK + 1,)),
            pltpu.SemaphoreType.DMA((NBLK,)),
            pltpu.SemaphoreType.DMA((NBLK,)),
        ],
        compiler_params=pltpu.CompilerParams(vmem_limit_bytes=VMEM_LIMIT),
        cost_estimate=pl.CostEstimate(flops=1 << 22, bytes_accessed=12 << 20, transcendentals=0),
        name="new_memory",
    )(info, keys, key_queue)


def with_targets(probe, target):
    digits = jnp.stack([target & 255, (target >> 8) & 255, target >> 16]).astype(bf16)
    digits = jnp.pad(digits, ((0, 13), (0, D - OWN)))
    return jnp.concatenate([probe, digits], axis=0)


def local_targets(q, first, core):
    d = q[:, OWN : OWN + 3, :OWN].astype(jnp.int32)
    t = d[:, 0] + d[:, 1] * 256 + d[:, 2] * 65536 - first
    t = jnp.where((t >= 0) & (t < 2 * SLOTS), t ^ (core * SLOTS), -1)
    return t.reshape(GRP)


def shards(events, w_in, w_out, probe, key_queue, target, pointer):
    core = lax.axis_index("c")
    chip = lax.axis_index("x") * SIZES[1] + lax.axis_index("z")
    first_slot = chip * (2 * SLOTS)

    q = with_targets(probe, target)
    partial = encode(events, w_in, w_out)
    k_other = swap_cores(key_queue)
    near = jnp.stack([q] + [shift(q, "zx", j) for j in (1, 2, 3)])
    parts = [partial] + [shift(partial, "ff", j) for j in (1, 3, 2)]
    far = [shift(near, "xz", j) for j in (1, 3, 2)]

    parts, near = lax.optimization_barrier((parts, near))
    far = [shift(near, "xz", j) for j in (1, 3, 2)]
    rolled = finish_keys(pointer, parts)
    all_keys = lax.all_gather(rolled, ("x", "z", "c"), axis=0, tiled=True)

    states = []
    for group in far + [near]:
        loc = local_targets(group, first_slot, core)
        if states:
            group, loc, states[-1] = lax.optimization_barrier((group, loc, states[-1]))
        states.append(attend(loc, group, key_queue, k_other))
    back = [shift(state, "xz", -j) for state, j in zip(states, (1, 3, 2))]
    pieces = merge([states[-1]] + back)
    arrived = [pieces[0]] + [shift(pieces[j], "zx", -j) for j in (1, 3, 2)]
    loss, grad = finish(probe, arrived)

    info = jnp.stack([pointer[0], chip * 2 + core]).astype(jnp.int32)
    new_memory = new_memory_of(info, all_keys, key_queue)
    return loss, grad, new_memory


def solution(mesh):
    fine = Mesh(mesh.devices.reshape(SIZES), ALL)
    mem = ("x", "z", "c")
    return jax.shard_map(
        shards,
        mesh=fine,
        in_specs=(
            P(mem, None, None),
            P(None, "f"),
            P("f", None),
            P(ALL, None),
            P(mem, None),
            P(ALL),
            P(),
        ),
        out_specs=(P(ALL), P(ALL, None), P(mem, None)),
        check_vma=False,
    )
```

```python
import functools

import jax
import jax.numpy as jnp
from jax import lax
from jax.experimental import pallas as pl
from jax.experimental.pallas import tpu as pltpu
from jax.sharding import Mesh
from jax.sharding import PartitionSpec as P

f32 = jnp.float32
bf16 = jnp.bfloat16
SOFT = 14.0
LOG2E = 1.4426950408889634
LN2 = 0.6931471805599453
C2 = SOFT * LOG2E
EPS = 1e-06
D = 256
EV = 32
OWN = 64
GRP = 256
SLOTS = 8192
SESS = 256
SIZES = (4, 4, 2, 4)
ALL = ("x", "z", "c", "f")
DIG = 64
REF = 80
PACK = 112
ML = 64
POS = 72
PIECE = 136
BIG = 2.0**90
CONTRACT_LAST = (((1,), (1,)), ((), ()))
VMEM_LIMIT = 62 << 20
PARAMS = pltpu.CompilerParams(vmem_limit_bytes=VMEM_LIMIT)
SMALL = pltpu.CompilerParams(vmem_limit_bytes=16 << 20)


def flat(p):
    return ((p[0] * SIZES[1] + p[1]) * SIZES[2] + p[2]) * SIZES[3] + p[3]


def ring(axes, step):
    pairs = []
    for x in range(SIZES[0]):
        for z in range(SIZES[1]):
            for c in range(SIZES[2]):
                for f in range(SIZES[3]):
                    p = [x, z, c, f]
                    k = "xzcf".index(axes[c])
                    p[k] = (p[k] + step) % SIZES[k]
                    pairs.append((flat((x, z, c, f)), flat(p)))
    return pairs


def shift(a, axes, step):
    return lax.ppermute(a, ALL, ring(axes, step % 4))


def swap_cores(a):
    return lax.ppermute(a, "c", [(0, 1), (1, 0)])


PARTS = 4
SUB = 8


def encoder_kernel(
    ev_ref, w_in_ref, w_out_ref, probe_ref, target_ref, k_ref, out_ref, pack_ref, evbuf, kbuf, pooled, sems
):
    step = SESS // PARTS

    def copy(n):
        rows = pl.ds(n * step, step)
        return pltpu.make_async_copy(ev_ref.at[rows], evbuf.at[rows], sems.at[n])

    sample = pltpu.make_async_copy(k_ref.at[pl.ds(0, 256)], kbuf, sems.at[PARTS])
    copy(0).start()
    sample.start()
    for n in range(1, PARTS):
        copy(n).start()

    pack_ref[:DIG, :] = probe_ref[...]
    target = target_ref[...]
    digits = [target & 255, (target >> 8) & 255, target >> 16]
    digits = jnp.concatenate([d.astype(f32) for d in digits] + [jnp.zeros((13, OWN), f32)], axis=0)
    digits = jnp.concatenate([digits, jnp.zeros((16, D - OWN), f32)], axis=1)
    pack_ref[DIG:REF, :] = digits.astype(bf16)
    sample.wait()
    s = lax.dot_general(probe_ref[...], kbuf[...], CONTRACT_LAST, preferred_element_type=f32)
    top = jnp.max(s, axis=1, keepdims=True) * C2
    top = jnp.broadcast_to(top - jnp.abs(top) * (1.0 / 256), (OWN, 128))
    pack_ref[REF:PACK, :] = jnp.concatenate([top[:32], top[32:]], axis=1).astype(bf16)

    def project(s):
        return jnp.dot(
            evbuf[s : s + SUB].reshape(SUB * EV, D), w_in_ref[...], preferred_element_type=f32
        )

    copy(0).wait()
    x = project(0)
    for s in range(0, SESS, SUB):
        if s + SUB < SESS:
            if (s + SUB) % step == 0:
                copy((s + SUB) // step).wait()
            following = project(s + SUB)
        inner = x * (0.7978845608028654 + 0.035677408136300125 * (x * x))
        g = x + x * jnp.tanh(inner)
        pooled[s : s + SUB, :] = jnp.sum(g.reshape(SUB, EV, D), axis=1) * (0.5 / EV)
        x = following
    out_ref[...] = jnp.dot(pooled[...].astype(bf16), w_out_ref[...], preferred_element_type=f32)


def encode(events, w_in, w_out, probe, target, key_queue):
    anywhere = pl.BlockSpec(memory_space=pl.ANY)
    inside = pl.BlockSpec(memory_space=pltpu.VMEM)
    return pl.pallas_call(
        encoder_kernel,
        in_specs=[anywhere, inside, inside, inside, inside, anywhere],
        out_specs=[inside, inside],
        out_shape=[
            jax.ShapeDtypeStruct((SESS, D), f32),
            jax.ShapeDtypeStruct((PACK, D), bf16),
        ],
        scratch_shapes=[
            pltpu.VMEM((SESS, EV, D), bf16),
            pltpu.VMEM((256, D), bf16),
            pltpu.VMEM((SESS, D), f32),
            pltpu.SemaphoreType.DMA((PARTS + 1,)),
        ],
        compiler_params=PARAMS,
        cost_estimate=pl.CostEstimate(
            flops=2 * SESS * EV * D * D, bytes_accessed=4 << 20, transcendentals=SESS * EV * D
        ),
        name="encoder",
    )(events, w_in, w_out, probe, target.reshape(1, OWN), key_queue)


def keys_kernel(ptr_ref, a_ref, b_ref, c_ref, d_ref, out_ref):
    raw = (a_ref[...] + b_ref[...]) + (c_ref[...] + d_ref[...])
    scale = lax.rsqrt(jnp.mean(raw * raw, axis=1, keepdims=True) + EPS)
    keys = (raw * scale / 16.0).astype(bf16)
    turn = lax.rem(ptr_ref[0], SESS)
    row = lax.broadcasted_iota(jnp.int32, (SESS, SESS), 0)
    col = lax.broadcasted_iota(jnp.int32, (SESS, SESS), 1)
    source = row - turn
    source = jnp.where(source < 0, source + SESS, source)
    pick = jnp.where(col == source, 1.0, 0.0).astype(bf16)
    out_ref[...] = jnp.dot(pick, keys, preferred_element_type=f32).astype(bf16)


def finish_keys(pointer, parts):
    return pl.pallas_call(
        keys_kernel,
        in_specs=[pl.BlockSpec(memory_space=pltpu.SMEM)]
        + [pl.BlockSpec(memory_space=pltpu.VMEM)] * 4,
        out_specs=pl.BlockSpec(memory_space=pltpu.VMEM),
        out_shape=jax.ShapeDtypeStruct((SESS, D), bf16),
        compiler_params=SMALL,
        cost_estimate=pl.CostEstimate(flops=1 << 26, bytes_accessed=2 << 20, transcendentals=0),
        name="finish_keys",
    )(pointer, *parts)


def diagonal(n):
    return lax.broadcasted_iota(jnp.int32, (n, n), 0) == lax.broadcasted_iota(
        jnp.int32, (n, n), 1
    )


def to_row(col, eye):
    return jnp.sum(jnp.where(eye, jnp.broadcast_to(col, eye.shape), 0.0), axis=0, keepdims=True)


def to_col(row, eye):
    return jnp.sum(jnp.where(eye, jnp.broadcast_to(row, eye.shape), 0.0), axis=1, keepdims=True)


SB = 512


def attend_kernel(n, info_ref, *refs):
    qs, (k0_ref, far_ref), outs = refs[:n], refs[n : n + 2], refs[n + 2 : 2 * n + 2]
    q2, m_ref, l_ref, acc, listed, todo, k1_ref, sems = refs[2 * n + 2 :]
    fill = pltpu.make_async_copy(far_ref, k1_ref, sems.at[n])
    fill.start()
    first_slot, core = info_ref[0].astype(f32), info_ref[1]

    copies = []
    row = lax.broadcasted_iota(jnp.int32, (GRP, GRP), 0)
    lane = lax.broadcasted_iota(jnp.int32, (GRP, GRP), 1)
    for g in range(n):
        at = []
        for j in range(4):
            d = qs[g][j, DIG:REF, :].astype(f32)
            at.append((d[0:1] + d[1:2] * 256.0 + d[2:3] * 65536.0)[:, :OWN])
        at = jnp.concatenate(at, axis=1) - first_slot
        inside = jnp.logical_and(at >= 0.0, at < 2.0 * SLOTS)
        flag = jnp.broadcast_to(jnp.where(inside, 1.0, 0.0), (GRP, GRP))
        before = jnp.sum(jnp.where(lane < row, flag, 0.0), axis=1, keepdims=True)
        upto = jnp.sum(jnp.where(lane <= row, flag, 0.0), axis=1, keepdims=True)
        slot = lane.astype(f32)
        goes = jnp.logical_and(before == slot, upto == slot + 1.0)
        turned = jnp.where(at < SLOTS, at + SLOTS, at - SLOTS)
        t = jnp.clip(jnp.where(core == 1, turned, at), 0.0, 2.0 * SLOTS - 1.0).astype(jnp.int32)
        values = jnp.concatenate(
            [lane[:1].astype(f32), (t & 255).astype(f32), (t >> 8).astype(f32), jnp.zeros((13, GRP), f32)],
            axis=0,
        )
        packed = jnp.dot(
            values.astype(bf16), jnp.where(goes, 1.0, 0.0).astype(bf16), preferred_element_type=f32
        )
        entry = packed[0:1] + packed[1:2] * 256.0 + packed[2:3] * 65536.0
        count = jnp.broadcast_to(upto[GRP - 1 : GRP, :], (1, GRP))
        listed[g, :, :] = jnp.concatenate([entry, count, jnp.zeros((6, GRP), f32)], axis=0).astype(
            jnp.int32
        )
        copy = pltpu.make_async_copy(listed.at[g], todo.at[g], sems.at[g])
        copy.start()
        copies.append(copy)

    for g in range(n):
        for j in range(4):
            at = g * GRP + j * OWN
            q2[at : at + OWN, :] = qs[g][j, :OWN, :]
            m_ref[at : at + 32, :] = qs[g][j, REF:PACK, :128].astype(f32)
            m_ref[at + 32 : at + OWN, :] = qs[g][j, REF:PACK, 128:].astype(f32)
    l_ref[...] = jnp.zeros_like(l_ref)
    acc[...] = jnp.zeros_like(acc)

    def score(g, k, b):
        return lax.dot_general(
            q2[g * GRP : (g + 1) * GRP, :],
            k[b : b + SB, :],
            CONTRACT_LAST,
            preferred_element_type=f32,
        )

    steps = [(g, k, b) for k in (k0_ref, k1_ref) for b in range(0, SLOTS, SB) for g in range(n)]
    s = score(*steps[0])
    for at, (g, k, b) in enumerate(steps):
        if at + 1 < len(steps):
            if at + 1 == len(steps) // 2:
                fill.wait()
            following = score(*steps[at + 1])
        rows = slice(g * GRP, (g + 1) * GRP)
        m = m_ref[rows, :]
        l = l_ref[rows, :]
        ps = []
        for j in range(0, SB, 128):
            p = jnp.exp2(s[:, j : j + 128] * C2 - m)
            l = l + p
            ps.append(p.astype(bf16))
        l_ref[rows, :] = l
        acc[rows, :] += jnp.dot(
            jnp.concatenate(ps, axis=1), k[b : b + SB, :], preferred_element_type=f32
        )
        s = following

    @pl.when(jnp.logical_not(jnp.max(l_ref[...]) < BIG))
    def _():
        m_ref[...] = jnp.full_like(m_ref, -3.0e38)
        l_ref[...] = jnp.zeros_like(l_ref)
        acc[...] = jnp.zeros_like(acc)

        def again(k, at, carry):
            block = k[pl.ds(pl.multiple_of(at * 256, 256), 256), :]
            for g in range(n):
                rows = slice(g * GRP, (g + 1) * GRP)
                t = C2 * lax.dot_general(
                    q2[rows, :], block, CONTRACT_LAST, preferred_element_type=f32
                )
                old = m_ref[rows, :]
                new = jnp.maximum(old, jnp.max(t, axis=1, keepdims=True))
                keep = jnp.exp2(old - new)
                p = jnp.exp2(t - new[:, :1])
                l_ref[rows, :] = l_ref[rows, :] * keep + (p[:, :128] + p[:, 128:])
                acc[rows, :] = acc[rows, :] * keep[:, :1] + jnp.dot(
                    p.astype(bf16), block, preferred_element_type=f32
                )
                m_ref[rows, :] = new
            return carry

        for k in (k0_ref, k1_ref):
            lax.fori_loop(0, SLOTS // 256, functools.partial(again, k), 0)

    eye = diagonal(OWN)
    lane_pad = jnp.zeros((1, D - OWN), f32)
    for g in range(n):
        out_ref = outs[g]
        for j in range(4):
            at = g * GRP + j * OWN
            rows = slice(at, at + OWN)
            out_ref[j, :OWN, :] = acc[rows, :]
            m_row = to_row(m_ref[rows, :1], eye)
            l_row = to_row(jnp.sum(l_ref[rows, :], axis=1, keepdims=True), eye)
            out_ref[j, ML:POS, :] = jnp.concatenate(
                [
                    jnp.concatenate([m_row, lane_pad], axis=1),
                    jnp.concatenate([l_row, lane_pad], axis=1),
                    jnp.zeros((6, D), f32),
                ],
                axis=0,
            )
            out_ref[j, POS:PIECE, :] = jnp.zeros((OWN, D), f32)

    row16 = lax.broadcasted_iota(jnp.int32, (16, D), 0)
    for g in range(n):
        out_ref = outs[g]
        copies[g].wait()

        def fetch(at, carry):
            entry = todo[g, 0, at]
            i = entry & (GRP - 1)
            t = entry >> 8
            rows = pl.ds(pl.multiple_of(((t & (SLOTS - 1)) >> 4) << 4, 16), 16)
            group = jnp.where(
                t < SLOTS, k0_ref[rows, :].astype(f32), k1_ref[rows, :].astype(f32)
            )
            out_ref[i >> 6, pl.ds(POS + (i & 63), 1), :] = jnp.sum(
                jnp.where(row16 == (t & 15), group, 0.0), axis=0, keepdims=True
            )
            return carry

        lax.fori_loop(0, todo[g, 1, 0], fetch, 0)


def attend(info, groups, k_own, k_other):
    n = len(groups)
    inside = pl.BlockSpec(memory_space=pltpu.VMEM)
    return pl.pallas_call(
        functools.partial(attend_kernel, n),
        in_specs=[pl.BlockSpec(memory_space=pltpu.SMEM)] + [inside] * (n + 1) + [pl.BlockSpec(memory_space=pl.ANY)],
        out_specs=[inside] * n,
        out_shape=[jax.ShapeDtypeStruct((4, PIECE, D), f32)] * n,
        scratch_shapes=[
            pltpu.VMEM((n * GRP, D), bf16),
            pltpu.VMEM((n * GRP, 128), f32),
            pltpu.VMEM((n * GRP, 128), f32),
            pltpu.VMEM((n * GRP, D), f32),
            pltpu.VMEM((n, 8, GRP), jnp.int32),
            pltpu.SMEM((n, 8, GRP), jnp.int32),
            pltpu.VMEM((SLOTS, D), bf16),
            pltpu.SemaphoreType.DMA((n + 1,)),
        ],
        compiler_params=pltpu.CompilerParams(vmem_limit_bytes=40 << 20),
        cost_estimate=pl.CostEstimate(
            flops=n * 8 * GRP * SLOTS * D,
            bytes_accessed=9 << 20,
            transcendentals=n * 2 * GRP * SLOTS,
        ),
        name="attend",
    )(info, *groups, k_own, k_other)


def combine(pieces, eye):
    ms = [p[ML : ML + 1, :OWN] for p in pieces]
    top = functools.reduce(jnp.maximum, ms)
    scales = [jnp.exp2(m - top) for m in ms]
    total = sum(p[ML + 1 : ML + 2, :OWN] * s for p, s in zip(pieces, scales))
    return top, scales, total


def merge_kernel(a_ref, b_ref, c_ref, d_ref, *outs):
    eye = diagonal(OWN)
    lane_pad = jnp.zeros((1, D - OWN), f32)
    for j in range(4):
        refs = [r.at[j] for r in (a_ref, b_ref, c_ref, d_ref)]
        top, scales, total = combine(refs, eye)
        o = outs[j]
        o[:OWN, :] = sum(r[:OWN, :] * to_col(s, eye) for r, s in zip(refs, scales))
        o[ML:POS, :] = jnp.concatenate(
            [
                jnp.concatenate([top, lane_pad], axis=1),
                jnp.concatenate([total, lane_pad], axis=1),
                jnp.zeros((6, D), f32),
            ],
            axis=0,
        )
        o[POS:PIECE, :] = sum(r[POS:PIECE, :] for r in refs)


def merge(states):
    return pl.pallas_call(
        merge_kernel,
        in_specs=[pl.BlockSpec(memory_space=pltpu.VMEM)] * 4,
        out_specs=[pl.BlockSpec(memory_space=pltpu.VMEM)] * 4,
        out_shape=[jax.ShapeDtypeStruct((PIECE, D), f32)] * 4,
        compiler_params=SMALL,
        cost_estimate=pl.CostEstimate(flops=1 << 22, bytes_accessed=3 << 20, transcendentals=4096),
        name="merge",
    )(*states)


def final_kernel(q_ref, a_ref, b_ref, c_ref, d_ref, loss_ref, grad_ref):
    eye = diagonal(OWN)
    refs = (a_ref, b_ref, c_ref, d_ref)
    top, scales, total = combine(refs, eye)
    inverse = 1.0 / total
    acc = sum(r[:OWN, :] * to_col(s * inverse, eye) for r, s in zip(refs, scales))
    positive = sum(r[POS:PIECE, :] for r in refs)
    grad_ref[...] = SOFT * (acc - positive)
    score = SOFT * jnp.sum(q_ref[...].astype(f32) * positive, axis=1, keepdims=True)
    loss_ref[...] = top * LN2 + jnp.log(total) - to_row(score, eye)


def finish(q, pieces):
    loss, grad = pl.pallas_call(
        final_kernel,
        in_specs=[pl.BlockSpec(memory_space=pltpu.VMEM)] * 5,
        out_specs=[pl.BlockSpec(memory_space=pltpu.VMEM)] * 2,
        out_shape=[jax.ShapeDtypeStruct((1, OWN), f32), jax.ShapeDtypeStruct((OWN, D), f32)],
        compiler_params=SMALL,
        cost_estimate=pl.CostEstimate(flops=1 << 20, bytes_accessed=1 << 20, transcendentals=1024),
        name="finish",
    )(q, *pieces)
    return loss.reshape(OWN), grad


BLK = SESS
NBLK = SLOTS // BLK


def memory_kernel(info_ref, *refs):
    pieces, k_ref, out_ref, (rbuf, kbuf, obuf, gsem, ksem, osem) = refs[:8], refs[8], refs[9], refs[10:]
    core, pointer, x, z = info_ref[1], info_ref[2], info_ref[3], info_ref[4]
    me = (x * SIZES[1] + z) * 2 + core
    r = lax.rem(pointer, SLOTS)
    first = lax.div(pointer, SLOTS)
    second = lax.rem(first + 1, 32)
    turn = lax.div(r, BLK)
    inner = lax.rem(r, BLK)
    is_first, is_second = me == first, me == second

    def needs_new(b):
        return jnp.logical_or(
            jnp.logical_and(is_first, (b + 1) * BLK > r), jnp.logical_and(is_second, b * BLK < r)
        )

    def needs_old(b):
        return jnp.logical_not(
            jnp.logical_or(
                jnp.logical_and(is_first, b * BLK >= r),
                jnp.logical_and(is_second, (b + 1) * BLK <= r),
            )
        )

    def new_copy(piece, block, slot):
        return pltpu.make_async_copy(
            piece.at[block],
            rbuf.at[pl.ds(pl.multiple_of(slot * BLK, BLK), BLK)],
            gsem.at[slot],
        )

    def new_wanted(slot):
        return jnp.logical_or(
            jnp.logical_and(slot > 0, needs_new(slot - 1)),
            jnp.logical_and(slot < NBLK, needs_new(slot)),
        )

    def old_copy(b):
        rows = pl.ds(b * BLK, BLK)
        return pltpu.make_async_copy(k_ref.at[rows], kbuf.at[rows], ksem.at[b])

    def out_copy(b):
        rows = pl.ds(b * BLK, BLK)
        return pltpu.make_async_copy(obuf.at[rows], out_ref.at[rows], osem.at[b])

    for at, piece in enumerate(pieces):
        from_core = core if at < 4 else 1 - core
        for block in range(4):
            outer, inner_at = (at % 4), block
            sx = jnp.where(from_core == 0, x - outer, x - inner_at) & 3
            sz = jnp.where(from_core == 0, z - inner_at, z - outer) & 3
            slot = ((sx * SIZES[1] + sz) * 2 + from_core + turn + 1) & (NBLK - 1)

            @pl.when(new_wanted(slot))
            def _():
                new_copy(piece, block, slot).start()

            @pl.when(jnp.logical_and(slot == 0, new_wanted(NBLK)))
            def _():
                new_copy(piece, block, NBLK).start()

    for b in range(NBLK):

        @pl.when(needs_old(b))
        def _():
            old_copy(b).start()

    @pl.when(new_wanted(0))
    def _():
        new_copy(pieces[0], 0, 0).wait()

    row = lax.broadcasted_iota(jnp.int32, (BLK, D), 0)
    for b in range(NBLK):

        @pl.when(new_wanted(b + 1))
        def _():
            new_copy(pieces[0], 0, b + 1).wait()

        @pl.when(needs_old(b))
        def _():
            old_copy(b).wait()

        rows = slice(b * BLK, (b + 1) * BLK)

        @pl.when(needs_new(b))
        def _():
            earlier = row < inner
            at = row + b * BLK
            take = jnp.logical_or(
                jnp.logical_and(is_first, at >= r), jnp.logical_and(is_second, at < r)
            )
            fresh = jnp.where(
                earlier,
                rbuf[rows, :].astype(f32),
                rbuf[(b + 1) * BLK : (b + 2) * BLK, :].astype(f32),
            )
            obuf[rows, :] = jnp.where(take, fresh, kbuf[rows, :].astype(f32)).astype(bf16)

        @pl.when(jnp.logical_not(needs_new(b)))
        def _():
            obuf[rows, :] = kbuf[rows, :]

        out_copy(b).start()
    for b in range(NBLK):
        out_copy(b).wait()


def new_memory_of(info, pieces, key_queue):
    anywhere = pl.BlockSpec(memory_space=pl.ANY)
    return pl.pallas_call(
        memory_kernel,
        in_specs=[pl.BlockSpec(memory_space=pltpu.SMEM)] + [anywhere] * 9,
        out_specs=anywhere,
        out_shape=jax.ShapeDtypeStruct((SLOTS, D), bf16),
        scratch_shapes=[
            pltpu.VMEM((SLOTS + BLK, D), bf16),
            pltpu.VMEM((SLOTS, D), bf16),
            pltpu.VMEM((SLOTS, D), bf16),
            pltpu.SemaphoreType.DMA((NBLK + 1,)),
            pltpu.SemaphoreType.DMA((NBLK,)),
            pltpu.SemaphoreType.DMA((NBLK,)),
        ],
        compiler_params=PARAMS,
        cost_estimate=pl.CostEstimate(flops=1 << 22, bytes_accessed=12 << 20, transcendentals=0),
        name="new_memory",
    )(info, *pieces, key_queue)


def shards(events, w_in, w_out, probe, key_queue, target, pointer):
    tie = lax.optimization_barrier
    x, z, core = lax.axis_index("x"), lax.axis_index("z"), lax.axis_index("c")
    first_slot = (x * SIZES[1] + z) * (2 * SLOTS)
    info = jnp.stack([first_slot, core, pointer[0], x, z]).astype(jnp.int32)

    k_other = swap_cores(key_queue)
    partial, pack = encode(events, w_in, w_out, probe, target, key_queue)
    k_other, partial, pack = tie((k_other, partial, pack))
    near = jnp.stack([pack] + [shift(pack, "zx", j) for j in (1, 2, 3)])
    parts = [partial] + [shift(partial, "ff", j) for j in (1, 3, 2)]
    far = [shift(near, "xz", j) for j in (1, 3, 2)]
    parts, far[0] = tie((parts, far[0]))

    rolled = finish_keys(pointer, parts)
    keys = jnp.stack([rolled] + [shift(rolled, "zx", j) for j in (1, 2, 3)])

    s1, s3 = attend(info, far[:2], key_queue, k_other)
    keys, far[2], s1, s3 = tie((keys, far[2], s1, s3))
    back = [shift(s1, "xz", -1), shift(s3, "xz", -3)]
    pieces = [keys] + [shift(keys, "xz", j) for j in (1, 2, 3)]
    (s2,) = attend(info, [far[2]], key_queue, k_other)
    near, s2 = tie((near, s2))
    back.append(shift(s2, "xz", -2))
    (mine,) = attend(info, [near], key_queue, k_other)
    pieces, mine = tie((pieces, mine))
    pieces = pieces + [swap_cores(p) for p in pieces]
    split = merge([mine] + back)
    arrived = [split[0]] + [shift(split[j], "zx", -j) for j in (1, 3, 2)]
    new_memory = new_memory_of(info, pieces, key_queue)
    arrived, new_memory = tie((arrived, new_memory))
    loss, grad = finish(probe, arrived)
    return loss, grad, new_memory


def solution(mesh):
    fine = Mesh(mesh.devices.reshape(SIZES), ALL)
    mem = ("x", "z", "c")
    return jax.shard_map(
        shards,
        mesh=fine,
        in_specs=(
            P(mem, None, None),
            P(None, "f"),
            P("f", None),
            P(ALL, None),
            P(mem, None),
            P(ALL),
            P(),
        ),
        out_specs=(P(ALL), P(ALL, None), P(mem, None)),
        check_vma=False,
    )
```

```python
import functools

import jax
import jax.numpy as jnp
from jax import lax
from jax.experimental import pallas as pl
from jax.experimental.pallas import tpu as pltpu
from jax.sharding import Mesh
from jax.sharding import PartitionSpec as P

f32 = jnp.float32
bf16 = jnp.bfloat16
SOFT = 14.0
LOG2E = 1.4426950408889634
LN2 = 0.6931471805599453
C2 = SOFT * LOG2E
EPS = 1e-06
D = 256
EV = 32
OWN = 64
GRP = 256
SLOTS = 8192
SESS = 256
SIZES = (4, 4, 2, 4)
ALL = ("x", "z", "c", "f")
DIG = 64
REF = 80
PACK = 112
ML = 64
POS = 72
PIECE = 136
BIG = 2.0**90
CONTRACT_LAST = (((1,), (1,)), ((), ()))
VMEM_LIMIT = 62 << 20
PARAMS = pltpu.CompilerParams(vmem_limit_bytes=VMEM_LIMIT)
SMALL = pltpu.CompilerParams(vmem_limit_bytes=16 << 20)


def flat(p):
    return ((p[0] * SIZES[1] + p[1]) * SIZES[2] + p[2]) * SIZES[3] + p[3]


def ring(axes, step):
    pairs = []
    for x in range(SIZES[0]):
        for z in range(SIZES[1]):
            for c in range(SIZES[2]):
                for f in range(SIZES[3]):
                    p = [x, z, c, f]
                    k = "xzcf".index(axes[c])
                    p[k] = (p[k] + step) % SIZES[k]
                    pairs.append((flat((x, z, c, f)), flat(p)))
    return pairs


def shift(a, axes, step):
    return lax.ppermute(a, ALL, ring(axes, step % 4))


def swap_cores(a):
    return lax.ppermute(a, "c", [(0, 1), (1, 0)])


PARTS = 4
SUB = 8


def encoder_kernel(
    ev_ref, w_in_ref, w_out_ref, probe_ref, target_ref, k_ref, out_ref, pack_ref, evbuf, kbuf, pooled, sems
):
    step = SESS // PARTS

    def copy(n):
        rows = pl.ds(n * step, step)
        return pltpu.make_async_copy(ev_ref.at[rows], evbuf.at[rows], sems.at[n])

    sample = pltpu.make_async_copy(k_ref.at[pl.ds(0, 256)], kbuf, sems.at[PARTS])
    copy(0).start()
    sample.start()
    for n in range(1, PARTS):
        copy(n).start()

    pack_ref[:DIG, :] = probe_ref[...]
    target = target_ref[...]
    digits = [target & 255, (target >> 8) & 255, target >> 16]
    digits = jnp.concatenate([d.astype(f32) for d in digits] + [jnp.zeros((13, OWN), f32)], axis=0)
    digits = jnp.concatenate([digits, jnp.zeros((16, D - OWN), f32)], axis=1)
    pack_ref[DIG:REF, :] = digits.astype(bf16)
    sample.wait()
    s = lax.dot_general(probe_ref[...], kbuf[...], CONTRACT_LAST, preferred_element_type=f32)
    top = jnp.max(s, axis=1, keepdims=True) * C2
    top = jnp.broadcast_to(top - jnp.abs(top) * (1.0 / 256), (OWN, 128))
    pack_ref[REF:PACK, :] = jnp.concatenate([top[:32], top[32:]], axis=1).astype(bf16)

    def project(s):
        return jnp.dot(
            evbuf[s : s + SUB].reshape(SUB * EV, D), w_in_ref[...], preferred_element_type=f32
        )

    copy(0).wait()
    x = project(0)
    for s in range(0, SESS, SUB):
        if s + SUB < SESS:
            if (s + SUB) % step == 0:
                copy((s + SUB) // step).wait()
            following = project(s + SUB)
        inner = x * (0.7978845608028654 + 0.035677408136300125 * (x * x))
        g = x + x * jnp.tanh(inner)
        pooled[s : s + SUB, :] = jnp.sum(g.reshape(SUB, EV, D), axis=1) * (0.5 / EV)
        x = following
    out_ref[...] = jnp.dot(pooled[...].astype(bf16), w_out_ref[...], preferred_element_type=f32)


def encode(events, w_in, w_out, probe, target, key_queue):
    anywhere = pl.BlockSpec(memory_space=pl.ANY)
    inside = pl.BlockSpec(memory_space=pltpu.VMEM)
    return pl.pallas_call(
        encoder_kernel,
        in_specs=[anywhere, inside, inside, inside, inside, anywhere],
        out_specs=[inside, inside],
        out_shape=[
            jax.ShapeDtypeStruct((SESS, D), f32),
            jax.ShapeDtypeStruct((PACK, D), bf16),
        ],
        scratch_shapes=[
            pltpu.VMEM((SESS, EV, D), bf16),
            pltpu.VMEM((256, D), bf16),
            pltpu.VMEM((SESS, D), f32),
            pltpu.SemaphoreType.DMA((PARTS + 1,)),
        ],
        compiler_params=PARAMS,
        cost_estimate=pl.CostEstimate(
            flops=2 * SESS * EV * D * D, bytes_accessed=4 << 20, transcendentals=SESS * EV * D
        ),
        name="encoder",
    )(events, w_in, w_out, probe, target.reshape(1, OWN), key_queue)


def keys_kernel(ptr_ref, a_ref, b_ref, c_ref, d_ref, out_ref):
    raw = (a_ref[...] + b_ref[...]) + (c_ref[...] + d_ref[...])
    scale = lax.rsqrt(jnp.mean(raw * raw, axis=1, keepdims=True) + EPS)
    keys = (raw * scale / 16.0).astype(bf16)
    turn = lax.rem(ptr_ref[0], SESS)
    row = lax.broadcasted_iota(jnp.int32, (SESS, SESS), 0)
    col = lax.broadcasted_iota(jnp.int32, (SESS, SESS), 1)
    source = row - turn
    source = jnp.where(source < 0, source + SESS, source)
    pick = jnp.where(col == source, 1.0, 0.0).astype(bf16)
    out_ref[...] = jnp.dot(pick, keys, preferred_element_type=f32).astype(bf16)


def finish_keys(pointer, parts):
    return pl.pallas_call(
        keys_kernel,
        in_specs=[pl.BlockSpec(memory_space=pltpu.SMEM)]
        + [pl.BlockSpec(memory_space=pltpu.VMEM)] * 4,
        out_specs=pl.BlockSpec(memory_space=pltpu.VMEM),
        out_shape=jax.ShapeDtypeStruct((SESS, D), bf16),
        compiler_params=SMALL,
        cost_estimate=pl.CostEstimate(flops=1 << 26, bytes_accessed=2 << 20, transcendentals=0),
        name="finish_keys",
    )(pointer, *parts)


def diagonal(n):
    return lax.broadcasted_iota(jnp.int32, (n, n), 0) == lax.broadcasted_iota(
        jnp.int32, (n, n), 1
    )


def to_row(col, eye):
    return jnp.sum(jnp.where(eye, jnp.broadcast_to(col, eye.shape), 0.0), axis=0, keepdims=True)


def to_col(row, eye):
    return jnp.sum(jnp.where(eye, jnp.broadcast_to(row, eye.shape), 0.0), axis=1, keepdims=True)


SB = 512


def attend_kernel(n, first, info_ref, *refs):
    qs, (k0_ref, far_ref), outs = refs[:n], refs[n : n + 2], refs[n + 2 : 2 * n + 2]
    refs = refs[2 * n + 2 :]
    if first:
        base = pltpu.make_async_copy(k0_ref, refs[0], refs[-1].at[n + 1])
        base.start()
        refs = refs[1:]
    q2, m_ref, l_ref, acc, listed, todo, k1_ref, sems = refs
    fill = pltpu.make_async_copy(far_ref, k1_ref, sems.at[n])
    fill.start()
    first_slot, core = info_ref[0].astype(f32), info_ref[1]

    copies = []
    row = lax.broadcasted_iota(jnp.int32, (GRP, GRP), 0)
    lane = lax.broadcasted_iota(jnp.int32, (GRP, GRP), 1)
    for g in range(n):
        at = []
        for j in range(4):
            d = qs[g][j, DIG:REF, :].astype(f32)
            at.append((d[0:1] + d[1:2] * 256.0 + d[2:3] * 65536.0)[:, :OWN])
        at = jnp.concatenate(at, axis=1) - first_slot
        inside = jnp.logical_and(at >= 0.0, at < 2.0 * SLOTS)
        flag = jnp.broadcast_to(jnp.where(inside, 1.0, 0.0), (GRP, GRP))
        before = jnp.sum(jnp.where(lane < row, flag, 0.0), axis=1, keepdims=True)
        upto = jnp.sum(jnp.where(lane <= row, flag, 0.0), axis=1, keepdims=True)
        slot = lane.astype(f32)
        goes = jnp.logical_and(before == slot, upto == slot + 1.0)
        turned = jnp.where(at < SLOTS, at + SLOTS, at - SLOTS)
        t = jnp.clip(jnp.where(core == 1, turned, at), 0.0, 2.0 * SLOTS - 1.0).astype(jnp.int32)
        values = jnp.concatenate(
            [lane[:1].astype(f32), (t & 255).astype(f32), (t >> 8).astype(f32), jnp.zeros((13, GRP), f32)],
            axis=0,
        )
        packed = jnp.dot(
            values.astype(bf16), jnp.where(goes, 1.0, 0.0).astype(bf16), preferred_element_type=f32
        )
        entry = packed[0:1] + packed[1:2] * 256.0 + packed[2:3] * 65536.0
        count = jnp.broadcast_to(upto[GRP - 1 : GRP, :], (1, GRP))
        listed[g, :, :] = jnp.concatenate([entry, count, jnp.zeros((6, GRP), f32)], axis=0).astype(
            jnp.int32
        )
        copy = pltpu.make_async_copy(listed.at[g], todo.at[g], sems.at[g])
        copy.start()
        copies.append(copy)

    for g in range(n):
        for j in range(4):
            at = g * GRP + j * OWN
            q2[at : at + OWN, :] = qs[g][j, :OWN, :]
            m_ref[at : at + 32, :] = qs[g][j, REF:PACK, :128].astype(f32)
            m_ref[at + 32 : at + OWN, :] = qs[g][j, REF:PACK, 128:].astype(f32)
    l_ref[...] = jnp.zeros_like(l_ref)
    acc[...] = jnp.zeros_like(acc)

    def score(g, k, b):
        return lax.dot_general(
            q2[g * GRP : (g + 1) * GRP, :],
            k[b : b + SB, :],
            CONTRACT_LAST,
            preferred_element_type=f32,
        )

    steps = [(g, k, b) for k in (k0_ref, k1_ref) for b in range(0, SLOTS, SB) for g in range(n)]
    s = score(*steps[0])
    for at, (g, k, b) in enumerate(steps):
        if at + 1 < len(steps):
            if at + 1 == len(steps) // 2:
                fill.wait()
            following = score(*steps[at + 1])
        rows = slice(g * GRP, (g + 1) * GRP)
        m = m_ref[rows, :]
        l = l_ref[rows, :]
        ps = []
        for j in range(0, SB, 128):
            p = jnp.exp2(s[:, j : j + 128] * C2 - m)
            l = l + p
            ps.append(p.astype(bf16))
        l_ref[rows, :] = l
        acc[rows, :] += jnp.dot(
            jnp.concatenate(ps, axis=1), k[b : b + SB, :], preferred_element_type=f32
        )
        s = following

    @pl.when(jnp.logical_not(jnp.max(l_ref[...]) < BIG))
    def _():
        m_ref[...] = jnp.full_like(m_ref, -3.0e38)
        l_ref[...] = jnp.zeros_like(l_ref)
        acc[...] = jnp.zeros_like(acc)

        def again(k, at, carry):
            block = k[pl.ds(pl.multiple_of(at * 256, 256), 256), :]
            for g in range(n):
                rows = slice(g * GRP, (g + 1) * GRP)
                t = C2 * lax.dot_general(
                    q2[rows, :], block, CONTRACT_LAST, preferred_element_type=f32
                )
                old = m_ref[rows, :]
                new = jnp.maximum(old, jnp.max(t, axis=1, keepdims=True))
                keep = jnp.exp2(old - new)
                p = jnp.exp2(t - new[:, :1])
                l_ref[rows, :] = l_ref[rows, :] * keep + (p[:, :128] + p[:, 128:])
                acc[rows, :] = acc[rows, :] * keep[:, :1] + jnp.dot(
                    p.astype(bf16), block, preferred_element_type=f32
                )
                m_ref[rows, :] = new
            return carry

        for k in (k0_ref, k1_ref):
            lax.fori_loop(0, SLOTS // 256, functools.partial(again, k), 0)

    eye = diagonal(OWN)
    lane_pad = jnp.zeros((1, D - OWN), f32)
    for g in range(n):
        out_ref = outs[g]
        for j in range(4):
            at = g * GRP + j * OWN
            rows = slice(at, at + OWN)
            out_ref[j, :OWN, :] = acc[rows, :]
            m_row = to_row(m_ref[rows, :1], eye)
            l_row = to_row(jnp.sum(l_ref[rows, :], axis=1, keepdims=True), eye)
            out_ref[j, ML:POS, :] = jnp.concatenate(
                [
                    jnp.concatenate([m_row, lane_pad], axis=1),
                    jnp.concatenate([l_row, lane_pad], axis=1),
                    jnp.zeros((6, D), f32),
                ],
                axis=0,
            )
            out_ref[j, POS:PIECE, :] = jnp.zeros((OWN, D), f32)

    row16 = lax.broadcasted_iota(jnp.int32, (16, D), 0)
    for g in range(n):
        out_ref = outs[g]
        copies[g].wait()

        def fetch(at, carry):
            entry = todo[g, 0, at]
            i = entry & (GRP - 1)
            t = entry >> 8
            rows = pl.ds(pl.multiple_of(((t & (SLOTS - 1)) >> 4) << 4, 16), 16)
            group = jnp.where(
                t < SLOTS, k0_ref[rows, :].astype(f32), k1_ref[rows, :].astype(f32)
            )
            out_ref[i >> 6, pl.ds(POS + (i & 63), 1), :] = jnp.sum(
                jnp.where(row16 == (t & 15), group, 0.0), axis=0, keepdims=True
            )
            return carry

        lax.fori_loop(0, todo[g, 1, 0], fetch, 0)
    if first:
        base.wait()


def attend(info, groups, k_own, k_other, first=False):
    n = len(groups)
    inside = pl.BlockSpec(memory_space=pltpu.VMEM)
    anywhere = pl.BlockSpec(memory_space=pl.ANY)
    return pl.pallas_call(
        functools.partial(attend_kernel, n, first),
        in_specs=[pl.BlockSpec(memory_space=pltpu.SMEM)]
        + [inside] * n
        + [inside, anywhere],
        out_specs=[inside] * n + [anywhere] * first,
        out_shape=[jax.ShapeDtypeStruct((4, PIECE, D), f32)] * n
        + [jax.ShapeDtypeStruct((SLOTS, D), bf16)] * first,
        scratch_shapes=[
            pltpu.VMEM((n * GRP, D), bf16),
            pltpu.VMEM((n * GRP, 128), f32),
            pltpu.VMEM((n * GRP, 128), f32),
            pltpu.VMEM((n * GRP, D), f32),
            pltpu.VMEM((n, 8, GRP), jnp.int32),
            pltpu.SMEM((n, 8, GRP), jnp.int32),
            pltpu.VMEM((SLOTS, D), bf16),
            pltpu.SemaphoreType.DMA((n + 2,)),
        ],
        compiler_params=pltpu.CompilerParams(vmem_limit_bytes=40 << 20),
        cost_estimate=pl.CostEstimate(
            flops=n * 8 * GRP * SLOTS * D,
            bytes_accessed=9 << 20,
            transcendentals=n * 2 * GRP * SLOTS,
        ),
        name="attend",
    )(info, *groups, k_own, k_other)


def combine(pieces, eye):
    ms = [p[ML : ML + 1, :OWN] for p in pieces]
    top = functools.reduce(jnp.maximum, ms)
    scales = [jnp.exp2(m - top) for m in ms]
    total = sum(p[ML + 1 : ML + 2, :OWN] * s for p, s in zip(pieces, scales))
    return top, scales, total


def merge_kernel(a_ref, b_ref, c_ref, d_ref, *outs):
    eye = diagonal(OWN)
    lane_pad = jnp.zeros((1, D - OWN), f32)
    for j in range(4):
        refs = [r.at[j] for r in (a_ref, b_ref, c_ref, d_ref)]
        top, scales, total = combine(refs, eye)
        o = outs[j]
        o[:OWN, :] = sum(r[:OWN, :] * to_col(s, eye) for r, s in zip(refs, scales))
        o[ML:POS, :] = jnp.concatenate(
            [
                jnp.concatenate([top, lane_pad], axis=1),
                jnp.concatenate([total, lane_pad], axis=1),
                jnp.zeros((6, D), f32),
            ],
            axis=0,
        )
        o[POS:PIECE, :] = sum(r[POS:PIECE, :] for r in refs)


def merge(states):
    return pl.pallas_call(
        merge_kernel,
        in_specs=[pl.BlockSpec(memory_space=pltpu.VMEM)] * 4,
        out_specs=[pl.BlockSpec(memory_space=pltpu.VMEM)] * 4,
        out_shape=[jax.ShapeDtypeStruct((PIECE, D), f32)] * 4,
        compiler_params=SMALL,
        cost_estimate=pl.CostEstimate(flops=1 << 22, bytes_accessed=3 << 20, transcendentals=4096),
        name="merge",
    )(*states)


def final_kernel(q_ref, a_ref, b_ref, c_ref, d_ref, loss_ref, grad_ref):
    eye = diagonal(OWN)
    refs = (a_ref, b_ref, c_ref, d_ref)
    top, scales, total = combine(refs, eye)
    inverse = 1.0 / total
    acc = sum(r[:OWN, :] * to_col(s * inverse, eye) for r, s in zip(refs, scales))
    positive = sum(r[POS:PIECE, :] for r in refs)
    grad_ref[...] = SOFT * (acc - positive)
    score = SOFT * jnp.sum(q_ref[...].astype(f32) * positive, axis=1, keepdims=True)
    loss_ref[...] = top * LN2 + jnp.log(total) - to_row(score, eye)


def finish(q, pieces):
    loss, grad = pl.pallas_call(
        final_kernel,
        in_specs=[pl.BlockSpec(memory_space=pltpu.VMEM)] * 5,
        out_specs=[pl.BlockSpec(memory_space=pltpu.VMEM)] * 2,
        out_shape=[jax.ShapeDtypeStruct((1, OWN), f32), jax.ShapeDtypeStruct((OWN, D), f32)],
        compiler_params=SMALL,
        cost_estimate=pl.CostEstimate(flops=1 << 20, bytes_accessed=1 << 20, transcendentals=1024),
        name="finish",
    )(q, *pieces)
    return loss.reshape(OWN), grad


BLK = SESS
NBLK = SLOTS // BLK


def memory_kernel(info_ref, *refs):
    pieces, out_ref, (rbuf, kbuf, obuf, gsem, ksem, osem) = refs[:8], refs[9], refs[10:]
    core, pointer, x, z = info_ref[1], info_ref[2], info_ref[3], info_ref[4]
    me = (x * SIZES[1] + z) * 2 + core
    r = lax.rem(pointer, SLOTS)
    first = lax.div(pointer, SLOTS)
    second = lax.rem(first + 1, 32)
    turn = lax.div(r, BLK)
    inner = lax.rem(r, BLK)
    is_first, is_second = me == first, me == second

    def needs_new(b):
        return jnp.logical_or(
            jnp.logical_and(is_first, (b + 1) * BLK > r), jnp.logical_and(is_second, b * BLK < r)
        )

    def needs_old(b):
        return jnp.logical_and(
            needs_new(b), jnp.logical_and(b * BLK < r, (b + 1) * BLK > r)
        )

    def new_copy(piece, block, slot):
        return pltpu.make_async_copy(
            piece.at[block],
            rbuf.at[pl.ds(pl.multiple_of(slot * BLK, BLK), BLK)],
            gsem.at[slot],
        )

    def new_wanted(slot):
        return jnp.logical_or(
            jnp.logical_and(slot > 0, needs_new(slot - 1)),
            jnp.logical_and(slot < NBLK, needs_new(slot)),
        )

    def old_copy(b):
        rows = pl.ds(b * BLK, BLK)
        return pltpu.make_async_copy(out_ref.at[rows], kbuf.at[rows], ksem.at[b])

    def out_copy(b):
        rows = pl.ds(b * BLK, BLK)
        return pltpu.make_async_copy(obuf.at[rows], out_ref.at[rows], osem.at[b])

    for at, piece in enumerate(pieces):
        from_core = core if at < 4 else 1 - core
        for block in range(4):
            outer, inner_at = (at % 4), block
            sx = jnp.where(from_core == 0, x - outer, x - inner_at) & 3
            sz = jnp.where(from_core == 0, z - inner_at, z - outer) & 3
            slot = ((sx * SIZES[1] + sz) * 2 + from_core + turn + 1) & (NBLK - 1)

            @pl.when(new_wanted(slot))
            def _():
                new_copy(piece, block, slot).start()

            @pl.when(jnp.logical_and(slot == 0, new_wanted(NBLK)))
            def _():
                new_copy(piece, block, NBLK).start()

    for b in range(NBLK):

        @pl.when(needs_old(b))
        def _():
            old_copy(b).start()

    @pl.when(new_wanted(0))
    def _():
        new_copy(pieces[0], 0, 0).wait()

    row = lax.broadcasted_iota(jnp.int32, (BLK, D), 0)
    for b in range(NBLK):

        @pl.when(new_wanted(b + 1))
        def _():
            new_copy(pieces[0], 0, b + 1).wait()

        @pl.when(needs_old(b))
        def _():
            old_copy(b).wait()

        rows = slice(b * BLK, (b + 1) * BLK)

        @pl.when(needs_new(b))
        def _():
            fresh = jnp.where(
                row < inner,
                rbuf[rows, :].astype(f32),
                rbuf[(b + 1) * BLK : (b + 2) * BLK, :].astype(f32),
            )
            obuf[rows, :] = fresh.astype(bf16)

        @pl.when(needs_old(b))
        def _():
            at = row + b * BLK
            take = jnp.logical_or(
                jnp.logical_and(is_first, at >= r), jnp.logical_and(is_second, at < r)
            )
            obuf[rows, :] = jnp.where(
                take, obuf[rows, :].astype(f32), kbuf[rows, :].astype(f32)
            ).astype(bf16)

        @pl.when(needs_new(b))
        def _():
            out_copy(b).start()

    for b in range(NBLK):

        @pl.when(needs_new(b))
        def _():
            out_copy(b).wait()


def new_memory_of(info, pieces, base):
    anywhere = pl.BlockSpec(memory_space=pl.ANY)
    return pl.pallas_call(
        memory_kernel,
        in_specs=[pl.BlockSpec(memory_space=pltpu.SMEM)] + [anywhere] * 9,
        out_specs=anywhere,
        out_shape=jax.ShapeDtypeStruct((SLOTS, D), bf16),
        scratch_shapes=[
            pltpu.VMEM((SLOTS + BLK, D), bf16),
            pltpu.VMEM((SLOTS, D), bf16),
            pltpu.VMEM((SLOTS, D), bf16),
            pltpu.SemaphoreType.DMA((NBLK + 1,)),
            pltpu.SemaphoreType.DMA((NBLK,)),
            pltpu.SemaphoreType.DMA((NBLK,)),
        ],
        compiler_params=pltpu.CompilerParams(vmem_limit_bytes=24 << 20),
        cost_estimate=pl.CostEstimate(flops=1 << 22, bytes_accessed=12 << 20, transcendentals=0),
        input_output_aliases={9: 0},
        name="new_memory",
    )(info, *pieces, base)


def shards(events, w_in, w_out, probe, key_queue, target, pointer):
    tie = lax.optimization_barrier
    x, z, core = lax.axis_index("x"), lax.axis_index("z"), lax.axis_index("c")
    first_slot = (x * SIZES[1] + z) * (2 * SLOTS)
    info = jnp.stack([first_slot, core, pointer[0], x, z]).astype(jnp.int32)

    k_other = swap_cores(key_queue)
    partial, pack = encode(events, w_in, w_out, probe, target, key_queue)
    k_other, partial, pack = tie((k_other, partial, pack))
    near = jnp.stack([pack] + [shift(pack, "zx", j) for j in (1, 2, 3)])
    parts = [partial] + [shift(partial, "ff", j) for j in (1, 3, 2)]
    far = [shift(near, "xz", j) for j in (1, 3, 2)]
    parts, far[0] = tie((parts, far[0]))

    rolled = finish_keys(pointer, parts)
    keys = jnp.stack([rolled] + [shift(rolled, "zx", j) for j in (1, 2, 3)])

    s1, s3, base = attend(info, far[:2], key_queue, k_other, first=True)
    keys, far[2], s1, s3 = tie((keys, far[2], s1, s3))
    back = [shift(s1, "xz", -1), shift(s3, "xz", -3)]
    pieces = [keys] + [shift(keys, "xz", j) for j in (1, 2, 3)]
    (s2,) = attend(info, [far[2]], key_queue, k_other)
    near, s2 = tie((near, s2))
    back.append(shift(s2, "xz", -2))
    (mine,) = attend(info, [near], key_queue, k_other)
    pieces, mine = tie((pieces, mine))
    pieces = pieces + [swap_cores(p) for p in pieces]
    split = merge([mine] + back)
    arrived = [split[0]] + [shift(split[j], "zx", -j) for j in (1, 3, 2)]
    new_memory = new_memory_of(info, pieces, base)
    arrived, new_memory = tie((arrived, new_memory))
    loss, grad = finish(probe, arrived)
    return loss, grad, new_memory


def solution(mesh):
    fine = Mesh(mesh.devices.reshape(SIZES), ALL)
    mem = ("x", "z", "c")
    return jax.shard_map(
        shards,
        mesh=fine,
        in_specs=(
            P(mem, None, None),
            P(None, "f"),
            P("f", None),
            P(ALL, None),
            P(mem, None),
            P(ALL),
            P(),
        ),
        out_specs=(P(ALL), P(ALL, None), P(mem, None)),
        check_vma=False,
    )
```

```python
import functools

import jax
import jax.numpy as jnp
from jax import lax
from jax.experimental import pallas as pl
from jax.experimental.pallas import tpu as pltpu
from jax.sharding import Mesh
from jax.sharding import PartitionSpec as P

f32 = jnp.float32
bf16 = jnp.bfloat16
SOFT = 14.0
LOG2E = 1.4426950408889634
LN2 = 0.6931471805599453
C2 = SOFT * LOG2E
EPS = 1e-06
D = 256
EV = 32
OWN = 64
GRP = 256
SLOTS = 8192
SESS = 256
SIZES = (4, 4, 2, 4)
ALL = ("x", "z", "c", "f")
DIG = 64
REF = 80
PACK = 112
ML = 64
POS = 72
PIECE = 136
BIG = 2.0**90
CONTRACT_LAST = (((1,), (1,)), ((), ()))
VMEM_LIMIT = 62 << 20
PARAMS = pltpu.CompilerParams(vmem_limit_bytes=VMEM_LIMIT)
SMALL = pltpu.CompilerParams(vmem_limit_bytes=16 << 20)


def flat(p):
    return ((p[0] * SIZES[1] + p[1]) * SIZES[2] + p[2]) * SIZES[3] + p[3]


def ring(axes, step):
    pairs = []
    for x in range(SIZES[0]):
        for z in range(SIZES[1]):
            for c in range(SIZES[2]):
                for f in range(SIZES[3]):
                    p = [x, z, c, f]
                    k = "xzcf".index(axes[c])
                    p[k] = (p[k] + step) % SIZES[k]
                    pairs.append((flat((x, z, c, f)), flat(p)))
    return pairs


def shift(a, axes, step):
    return lax.ppermute(a, ALL, ring(axes, step % 4))


def swap_cores(a):
    return lax.ppermute(a, "c", [(0, 1), (1, 0)])


PARTS = 4
SUB = 8


def encoder_kernel(
    ev_ref, w_in_ref, w_out_ref, probe_ref, target_ref, k_ref, out_ref, pack_ref, evbuf, kbuf, pooled, sems
):
    step = SESS // PARTS

    def copy(n):
        rows = pl.ds(n * step, step)
        return pltpu.make_async_copy(ev_ref.at[rows], evbuf.at[rows], sems.at[n])

    sample = pltpu.make_async_copy(k_ref.at[pl.ds(0, 256)], kbuf, sems.at[PARTS])
    copy(0).start()
    sample.start()
    for n in range(1, PARTS):
        copy(n).start()

    pack_ref[:DIG, :] = probe_ref[...]
    target = target_ref[...]
    digits = [target & 255, (target >> 8) & 255, target >> 16]
    digits = jnp.concatenate([d.astype(f32) for d in digits] + [jnp.zeros((13, OWN), f32)], axis=0)
    digits = jnp.concatenate([digits, jnp.zeros((16, D - OWN), f32)], axis=1)
    pack_ref[DIG:REF, :] = digits.astype(bf16)
    sample.wait()
    s = lax.dot_general(probe_ref[...], kbuf[...], CONTRACT_LAST, preferred_element_type=f32)
    top = jnp.max(s, axis=1, keepdims=True) * C2
    top = jnp.broadcast_to(top - jnp.abs(top) * (1.0 / 256), (OWN, 128))
    pack_ref[REF:PACK, :] = jnp.concatenate([top[:32], top[32:]], axis=1).astype(bf16)

    def project(s):
        return jnp.dot(
            evbuf[s : s + SUB].reshape(SUB * EV, D), w_in_ref[...], preferred_element_type=f32
        )

    copy(0).wait()
    x = project(0)
    for s in range(0, SESS, SUB):
        if s + SUB < SESS:
            if (s + SUB) % step == 0:
                copy((s + SUB) // step).wait()
            following = project(s + SUB)
        inner = x * (0.7978845608028654 + 0.035677408136300125 * (x * x))
        g = x + x * jnp.tanh(inner)
        pooled[s : s + SUB, :] = jnp.sum(g.reshape(SUB, EV, D), axis=1) * (0.5 / EV)
        x = following
    out_ref[...] = jnp.dot(pooled[...].astype(bf16), w_out_ref[...], preferred_element_type=f32)


def encode(events, w_in, w_out, probe, target, key_queue):
    anywhere = pl.BlockSpec(memory_space=pl.ANY)
    inside = pl.BlockSpec(memory_space=pltpu.VMEM)
    return pl.pallas_call(
        encoder_kernel,
        in_specs=[anywhere, inside, inside, inside, inside, anywhere],
        out_specs=[inside, inside],
        out_shape=[
            jax.ShapeDtypeStruct((SESS, D), f32),
            jax.ShapeDtypeStruct((PACK, D), bf16),
        ],
        scratch_shapes=[
            pltpu.VMEM((SESS, EV, D), bf16),
            pltpu.VMEM((256, D), bf16),
            pltpu.VMEM((SESS, D), f32),
            pltpu.SemaphoreType.DMA((PARTS + 1,)),
        ],
        compiler_params=PARAMS,
        cost_estimate=pl.CostEstimate(
            flops=2 * SESS * EV * D * D, bytes_accessed=4 << 20, transcendentals=SESS * EV * D
        ),
        name="encoder",
    )(events, w_in, w_out, probe, target.reshape(1, OWN), key_queue)


def keys_kernel(ptr_ref, a_ref, b_ref, c_ref, d_ref, out_ref):
    raw = (a_ref[...] + b_ref[...]) + (c_ref[...] + d_ref[...])
    scale = lax.rsqrt(jnp.mean(raw * raw, axis=1, keepdims=True) + EPS)
    keys = (raw * scale / 16.0).astype(bf16)
    turn = lax.rem(ptr_ref[0], SESS)
    row = lax.broadcasted_iota(jnp.int32, (SESS, SESS), 0)
    col = lax.broadcasted_iota(jnp.int32, (SESS, SESS), 1)
    source = row - turn
    source = jnp.where(source < 0, source + SESS, source)
    pick = jnp.where(col == source, 1.0, 0.0).astype(bf16)
    out_ref[...] = jnp.dot(pick, keys, preferred_element_type=f32).astype(bf16)


def finish_keys(pointer, parts):
    return pl.pallas_call(
        keys_kernel,
        in_specs=[pl.BlockSpec(memory_space=pltpu.SMEM)]
        + [pl.BlockSpec(memory_space=pltpu.VMEM)] * 4,
        out_specs=pl.BlockSpec(memory_space=pltpu.VMEM),
        out_shape=jax.ShapeDtypeStruct((SESS, D), bf16),
        compiler_params=SMALL,
        cost_estimate=pl.CostEstimate(flops=1 << 26, bytes_accessed=2 << 20, transcendentals=0),
        name="finish_keys",
    )(pointer, *parts)


def diagonal(n):
    return lax.broadcasted_iota(jnp.int32, (n, n), 0) == lax.broadcasted_iota(
        jnp.int32, (n, n), 1
    )


def to_row(col, eye):
    return jnp.sum(jnp.where(eye, jnp.broadcast_to(col, eye.shape), 0.0), axis=0, keepdims=True)


def to_col(row, eye):
    return jnp.sum(jnp.where(eye, jnp.broadcast_to(row, eye.shape), 0.0), axis=1, keepdims=True)


SB = 512


def attend_kernel(n, first, info_ref, *refs):
    qs, (k0_ref, far_ref), outs = refs[:n], refs[n : n + 2], refs[n + 2 : 2 * n + 2]
    refs = refs[2 * n + 2 :]
    if first:
        base = pltpu.make_async_copy(k0_ref, refs[0], refs[-1].at[n + 1])
        base.start()
        refs = refs[1:]
    q2, m_ref, l_ref, acc, listed, todo, k1_ref, sems = refs
    fill = pltpu.make_async_copy(far_ref, k1_ref, sems.at[n])
    fill.start()
    first_slot, core = info_ref[0].astype(f32), info_ref[1]

    copies = []
    row = lax.broadcasted_iota(jnp.int32, (GRP, GRP), 0)
    lane = lax.broadcasted_iota(jnp.int32, (GRP, GRP), 1)
    for g in range(n):
        at = []
        for j in range(4):
            d = qs[g][j, DIG:REF, :].astype(f32)
            at.append((d[0:1] + d[1:2] * 256.0 + d[2:3] * 65536.0)[:, :OWN])
        at = jnp.concatenate(at, axis=1) - first_slot
        inside = jnp.logical_and(at >= 0.0, at < 2.0 * SLOTS)
        flag = jnp.broadcast_to(jnp.where(inside, 1.0, 0.0), (GRP, GRP))
        before = jnp.sum(jnp.where(lane < row, flag, 0.0), axis=1, keepdims=True)
        upto = jnp.sum(jnp.where(lane <= row, flag, 0.0), axis=1, keepdims=True)
        slot = lane.astype(f32)
        goes = jnp.logical_and(before == slot, upto == slot + 1.0)
        turned = jnp.where(at < SLOTS, at + SLOTS, at - SLOTS)
        t = jnp.clip(jnp.where(core == 1, turned, at), 0.0, 2.0 * SLOTS - 1.0).astype(jnp.int32)
        values = jnp.concatenate(
            [lane[:1].astype(f32), (t & 255).astype(f32), (t >> 8).astype(f32), jnp.zeros((13, GRP), f32)],
            axis=0,
        )
        packed = jnp.dot(
            values.astype(bf16), jnp.where(goes, 1.0, 0.0).astype(bf16), preferred_element_type=f32
        )
        entry = packed[0:1] + packed[1:2] * 256.0 + packed[2:3] * 65536.0
        count = jnp.broadcast_to(upto[GRP - 1 : GRP, :], (1, GRP))
        listed[g, :, :] = jnp.concatenate([entry, count, jnp.zeros((6, GRP), f32)], axis=0).astype(
            jnp.int32
        )
        copy = pltpu.make_async_copy(listed.at[g], todo.at[g], sems.at[g])
        copy.start()
        copies.append(copy)

    for g in range(n):
        for j in range(4):
            at = g * GRP + j * OWN
            q2[at : at + OWN, :] = qs[g][j, :OWN, :]
            m_ref[at : at + 32, :] = qs[g][j, REF:PACK, :128].astype(f32)
            m_ref[at + 32 : at + OWN, :] = qs[g][j, REF:PACK, 128:].astype(f32)
    l_ref[...] = jnp.zeros_like(l_ref)
    acc[...] = jnp.zeros_like(acc)

    def score(g, k, b):
        return lax.dot_general(
            q2[g * GRP : (g + 1) * GRP, :],
            k[b : b + SB, :],
            CONTRACT_LAST,
            preferred_element_type=f32,
        )

    steps = [(g, k, b) for k in (k0_ref, k1_ref) for b in range(0, SLOTS, SB) for g in range(n)]
    s = score(*steps[0])
    for at, (g, k, b) in enumerate(steps):
        if at + 1 < len(steps):
            if at + 1 == len(steps) // 2:
                fill.wait()
            following = score(*steps[at + 1])
        rows = slice(g * GRP, (g + 1) * GRP)
        m = m_ref[rows, :]
        l = l_ref[rows, :]
        ps = []
        for j in range(0, SB, 128):
            p = jnp.exp2(s[:, j : j + 128] * C2 - m)
            l = l + p
            ps.append(p.astype(bf16))
        l_ref[rows, :] = l
        acc[rows, :] += jnp.dot(
            jnp.concatenate(ps, axis=1), k[b : b + SB, :], preferred_element_type=f32
        )
        s = following

    @pl.when(jnp.logical_not(jnp.max(l_ref[...]) < BIG))
    def _():
        m_ref[...] = jnp.full_like(m_ref, -3.0e38)
        l_ref[...] = jnp.zeros_like(l_ref)
        acc[...] = jnp.zeros_like(acc)

        def again(k, at, carry):
            block = k[pl.ds(pl.multiple_of(at * 256, 256), 256), :]
            for g in range(n):
                rows = slice(g * GRP, (g + 1) * GRP)
                t = C2 * lax.dot_general(
                    q2[rows, :], block, CONTRACT_LAST, preferred_element_type=f32
                )
                old = m_ref[rows, :]
                new = jnp.maximum(old, jnp.max(t, axis=1, keepdims=True))
                keep = jnp.exp2(old - new)
                p = jnp.exp2(t - new[:, :1])
                l_ref[rows, :] = l_ref[rows, :] * keep + (p[:, :128] + p[:, 128:])
                acc[rows, :] = acc[rows, :] * keep[:, :1] + jnp.dot(
                    p.astype(bf16), block, preferred_element_type=f32
                )
                m_ref[rows, :] = new
            return carry

        for k in (k0_ref, k1_ref):
            lax.fori_loop(0, SLOTS // 256, functools.partial(again, k), 0)

    eye = diagonal(OWN)
    lane_pad = jnp.zeros((1, D - OWN), f32)
    for g in range(n):
        out_ref = outs[g]
        for j in range(4):
            at = g * GRP + j * OWN
            rows = slice(at, at + OWN)
            out_ref[j, :OWN, :] = acc[rows, :]
            m_row = to_row(m_ref[rows, :1], eye)
            l_row = to_row(jnp.sum(l_ref[rows, :], axis=1, keepdims=True), eye)
            out_ref[j, ML:POS, :] = jnp.concatenate(
                [
                    jnp.concatenate([m_row, lane_pad], axis=1),
                    jnp.concatenate([l_row, lane_pad], axis=1),
                    jnp.zeros((6, D), f32),
                ],
                axis=0,
            )
            out_ref[j, POS:PIECE, :] = jnp.zeros((OWN, D), f32)

    row16 = lax.broadcasted_iota(jnp.int32, (16, D), 0)
    for g in range(n):
        out_ref = outs[g]
        copies[g].wait()

        def fetch(at, carry):
            entry = todo[g, 0, at]
            i = entry & (GRP - 1)
            t = entry >> 8
            rows = pl.ds(pl.multiple_of(((t & (SLOTS - 1)) >> 4) << 4, 16), 16)
            group = jnp.where(
                t < SLOTS, k0_ref[rows, :].astype(f32), k1_ref[rows, :].astype(f32)
            )
            out_ref[i >> 6, pl.ds(POS + (i & 63), 1), :] = jnp.sum(
                jnp.where(row16 == (t & 15), group, 0.0), axis=0, keepdims=True
            )
            return carry

        lax.fori_loop(0, todo[g, 1, 0], fetch, 0)
    if first:
        base.wait()


def attend(info, groups, k_own, k_other, first=False):
    n = len(groups)
    inside = pl.BlockSpec(memory_space=pltpu.VMEM)
    anywhere = pl.BlockSpec(memory_space=pl.ANY)
    return pl.pallas_call(
        functools.partial(attend_kernel, n, first),
        in_specs=[pl.BlockSpec(memory_space=pltpu.SMEM)]
        + [inside] * n
        + [inside, anywhere],
        out_specs=[inside] * n + [anywhere] * first,
        out_shape=[jax.ShapeDtypeStruct((4, PIECE, D), f32)] * n
        + [jax.ShapeDtypeStruct((SLOTS, D), bf16)] * first,
        scratch_shapes=[
            pltpu.VMEM((n * GRP, D), bf16),
            pltpu.VMEM((n * GRP, 128), f32),
            pltpu.VMEM((n * GRP, 128), f32),
            pltpu.VMEM((n * GRP, D), f32),
            pltpu.VMEM((n, 8, GRP), jnp.int32),
            pltpu.SMEM((n, 8, GRP), jnp.int32),
            pltpu.VMEM((SLOTS, D), bf16),
            pltpu.SemaphoreType.DMA((n + 2,)),
        ],
        compiler_params=pltpu.CompilerParams(vmem_limit_bytes=40 << 20),
        cost_estimate=pl.CostEstimate(
            flops=n * 8 * GRP * SLOTS * D,
            bytes_accessed=9 << 20,
            transcendentals=n * 2 * GRP * SLOTS,
        ),
        name="attend",
    )(info, *groups, k_own, k_other)


def combine(pieces, eye):
    ms = [p[ML : ML + 1, :OWN] for p in pieces]
    top = functools.reduce(jnp.maximum, ms)
    scales = [jnp.exp2(m - top) for m in ms]
    total = sum(p[ML + 1 : ML + 2, :OWN] * s for p, s in zip(pieces, scales))
    return top, scales, total


def merge_kernel(a_ref, b_ref, c_ref, d_ref, *outs):
    eye = diagonal(OWN)
    lane_pad = jnp.zeros((1, D - OWN), f32)
    for j in range(4):
        refs = [r.at[j] for r in (a_ref, b_ref, c_ref, d_ref)]
        top, scales, total = combine(refs, eye)
        o = outs[j]
        o[:OWN, :] = sum(r[:OWN, :] * to_col(s, eye) for r, s in zip(refs, scales))
        o[ML:POS, :] = jnp.concatenate(
            [
                jnp.concatenate([top, lane_pad], axis=1),
                jnp.concatenate([total, lane_pad], axis=1),
                jnp.zeros((6, D), f32),
            ],
            axis=0,
        )
        o[POS:PIECE, :] = sum(r[POS:PIECE, :] for r in refs)


def merge(states):
    return pl.pallas_call(
        merge_kernel,
        in_specs=[pl.BlockSpec(memory_space=pltpu.VMEM)] * 4,
        out_specs=[pl.BlockSpec(memory_space=pltpu.VMEM)] * 4,
        out_shape=[jax.ShapeDtypeStruct((PIECE, D), f32)] * 4,
        compiler_params=SMALL,
        cost_estimate=pl.CostEstimate(flops=1 << 22, bytes_accessed=3 << 20, transcendentals=4096),
        name="merge",
    )(*states)


def final_kernel(q_ref, a_ref, b_ref, c_ref, d_ref, loss_ref, grad_ref):
    eye = diagonal(OWN)
    refs = (a_ref, b_ref, c_ref, d_ref)
    top, scales, total = combine(refs, eye)
    inverse = 1.0 / total
    acc = sum(r[:OWN, :] * to_col(s * inverse, eye) for r, s in zip(refs, scales))
    positive = sum(r[POS:PIECE, :] for r in refs)
    grad_ref[...] = SOFT * (acc - positive)
    score = SOFT * jnp.sum(q_ref[...].astype(f32) * positive, axis=1, keepdims=True)
    loss_ref[...] = top * LN2 + jnp.log(total) - to_row(score, eye)


def finish(q, pieces):
    loss, grad = pl.pallas_call(
        final_kernel,
        in_specs=[pl.BlockSpec(memory_space=pltpu.VMEM)] * 5,
        out_specs=[pl.BlockSpec(memory_space=pltpu.VMEM)] * 2,
        out_shape=[jax.ShapeDtypeStruct((1, OWN), f32), jax.ShapeDtypeStruct((OWN, D), f32)],
        compiler_params=SMALL,
        cost_estimate=pl.CostEstimate(flops=1 << 20, bytes_accessed=1 << 20, transcendentals=1024),
        name="finish",
    )(q, *pieces)
    return loss.reshape(OWN), grad


BLK = SESS
NBLK = SLOTS // BLK


def memory_kernel(info_ref, *refs):
    pieces, out_ref, (rbuf, kbuf, obuf, gsem, ksem, osem) = refs[:8], refs[9], refs[10:]
    core, pointer, x, z = info_ref[1], info_ref[2], info_ref[3], info_ref[4]
    me = (x * SIZES[1] + z) * 2 + core
    r = lax.rem(pointer, SLOTS)
    first = lax.div(pointer, SLOTS)
    second = lax.rem(first + 1, 32)
    turn = lax.div(r, BLK)
    inner = lax.rem(r, BLK)
    is_first, is_second = me == first, me == second

    def needs_new(b):
        return jnp.logical_or(
            jnp.logical_and(is_first, (b + 1) * BLK > r), jnp.logical_and(is_second, b * BLK < r)
        )

    def needs_old(b):
        return jnp.logical_and(
            needs_new(b), jnp.logical_and(b * BLK < r, (b + 1) * BLK > r)
        )

    def new_copy(piece, block, slot):
        return pltpu.make_async_copy(
            piece.at[block],
            rbuf.at[pl.ds(pl.multiple_of(slot * BLK, BLK), BLK)],
            gsem.at[slot],
        )

    def new_wanted(slot):
        return jnp.logical_or(
            jnp.logical_and(slot > 0, needs_new(slot - 1)),
            jnp.logical_and(slot < NBLK, needs_new(slot)),
        )

    def old_copy(b):
        rows = pl.ds(b * BLK, BLK)
        return pltpu.make_async_copy(out_ref.at[rows], kbuf.at[rows], ksem.at[b])

    def out_copy(b):
        rows = pl.ds(b * BLK, BLK)
        return pltpu.make_async_copy(obuf.at[rows], out_ref.at[rows], osem.at[b])

    for at, piece in enumerate(pieces):
        from_core = core if at < 4 else 1 - core
        for block in range(4):
            outer, inner_at = (at % 4), block
            sx = jnp.where(from_core == 0, x - outer, x - inner_at) & 3
            sz = jnp.where(from_core == 0, z - inner_at, z - outer) & 3
            slot = ((sx * SIZES[1] + sz) * 2 + from_core + turn + 1) & (NBLK - 1)

            @pl.when(new_wanted(slot))
            def _():
                new_copy(piece, block, slot).start()

            @pl.when(jnp.logical_and(slot == 0, new_wanted(NBLK)))
            def _():
                new_copy(piece, block, NBLK).start()

    for b in range(NBLK):

        @pl.when(needs_old(b))
        def _():
            old_copy(b).start()

    @pl.when(new_wanted(0))
    def _():
        new_copy(pieces[0], 0, 0).wait()

    row = lax.broadcasted_iota(jnp.int32, (BLK, D), 0)
    whole = lax.div(inner, 16)
    starts = [jnp.where(t < whole, 0, BLK) + t * 16 for t in range(BLK // 16)]
    for b in range(NBLK):

        @pl.when(new_wanted(b + 1))
        def _():
            new_copy(pieces[0], 0, b + 1).wait()

        @pl.when(needs_old(b))
        def _():
            old_copy(b).wait()

        rows = slice(b * BLK, (b + 1) * BLK)

        @pl.when(needs_new(b))
        def _():
            for t in range(BLK // 16):
                source = pl.ds(pl.multiple_of(starts[t] + b * BLK, 16), 16)
                obuf[b * BLK + t * 16 : b * BLK + t * 16 + 16, :] = rbuf[source, :]
            at = pl.multiple_of(b * BLK + whole * 16, 16)
            later = pl.multiple_of(b * BLK + whole * 16 + BLK, 16)
            obuf[pl.ds(at, 16), :] = jnp.where(
                row[:16] < inner - whole * 16,
                rbuf[pl.ds(at, 16), :].astype(f32),
                rbuf[pl.ds(later, 16), :].astype(f32),
            ).astype(bf16)

        @pl.when(needs_old(b))
        def _():
            at = row + b * BLK
            take = jnp.logical_or(
                jnp.logical_and(is_first, at >= r), jnp.logical_and(is_second, at < r)
            )
            obuf[rows, :] = jnp.where(
                take, obuf[rows, :].astype(f32), kbuf[rows, :].astype(f32)
            ).astype(bf16)

        @pl.when(needs_new(b))
        def _():
            out_copy(b).start()

    for b in range(NBLK):

        @pl.when(needs_new(b))
        def _():
            out_copy(b).wait()


def new_memory_of(info, pieces, base):
    anywhere = pl.BlockSpec(memory_space=pl.ANY)
    return pl.pallas_call(
        memory_kernel,
        in_specs=[pl.BlockSpec(memory_space=pltpu.SMEM)] + [anywhere] * 9,
        out_specs=anywhere,
        out_shape=jax.ShapeDtypeStruct((SLOTS, D), bf16),
        scratch_shapes=[
            pltpu.VMEM((SLOTS + BLK, D), bf16),
            pltpu.VMEM((SLOTS, D), bf16),
            pltpu.VMEM((SLOTS, D), bf16),
            pltpu.SemaphoreType.DMA((NBLK + 1,)),
            pltpu.SemaphoreType.DMA((NBLK,)),
            pltpu.SemaphoreType.DMA((NBLK,)),
        ],
        compiler_params=pltpu.CompilerParams(vmem_limit_bytes=24 << 20),
        cost_estimate=pl.CostEstimate(flops=1 << 22, bytes_accessed=12 << 20, transcendentals=0),
        input_output_aliases={9: 0},
        name="new_memory",
    )(info, *pieces, base)


def shards(events, w_in, w_out, probe, key_queue, target, pointer):
    tie = lax.optimization_barrier
    x, z, core = lax.axis_index("x"), lax.axis_index("z"), lax.axis_index("c")
    first_slot = (x * SIZES[1] + z) * (2 * SLOTS)
    info = jnp.stack([first_slot, core, pointer[0], x, z]).astype(jnp.int32)

    k_other = swap_cores(key_queue)
    partial, pack = encode(events, w_in, w_out, probe, target, key_queue)
    k_other, partial, pack = tie((k_other, partial, pack))
    near = jnp.stack([pack] + [shift(pack, "zx", j) for j in (1, 2, 3)])
    parts = [partial] + [shift(partial, "ff", j) for j in (1, 3, 2)]
    far = [shift(near, "xz", j) for j in (1, 3, 2)]
    parts, far[0] = tie((parts, far[0]))

    rolled = finish_keys(pointer, parts)
    keys = jnp.stack([rolled] + [shift(rolled, "zx", j) for j in (1, 2, 3)])

    s1, s3, base = attend(info, far[:2], key_queue, k_other, first=True)
    keys, far[2], s1, s3 = tie((keys, far[2], s1, s3))
    back = [shift(s1, "xz", -1), shift(s3, "xz", -3)]
    pieces = [keys] + [shift(keys, "xz", j) for j in (1, 2, 3)]
    (s2,) = attend(info, [far[2]], key_queue, k_other)
    near, s2 = tie((near, s2))
    back.append(shift(s2, "xz", -2))
    (mine,) = attend(info, [near], key_queue, k_other)
    pieces, mine = tie((pieces, mine))
    pieces = pieces + [swap_cores(p) for p in pieces]
    split = merge([mine] + back)
    arrived = [split[0]] + [shift(split[j], "zx", -j) for j in (1, 3, 2)]
    new_memory = new_memory_of(info, pieces, base)
    arrived, new_memory = tie((arrived, new_memory))
    loss, grad = finish(probe, arrived)
    return loss, grad, new_memory


def solution(mesh):
    fine = Mesh(mesh.devices.reshape(SIZES), ALL)
    mem = ("x", "z", "c")
    return jax.shard_map(
        shards,
        mesh=fine,
        in_specs=(
            P(mem, None, None),
            P(None, "f"),
            P("f", None),
            P(ALL, None),
            P(mem, None),
            P(ALL),
            P(),
        ),
        out_specs=(P(ALL), P(ALL, None), P(mem, None)),
        check_vma=False,
    )
```
